256 devices in a mesh: morton: 128 (over z, x, y), dp: 2 (over core).
Axes of the slice: x: 4, y: 4, z: 8, core: 2. Of those that a mesh axis runs over, the one named last changes fastest.
Arguments:
- node_feat: bfloat16 [2, 65536, 128], P('dp', 'morton'), may hold values from -6 to 6
- edge_feat: bfloat16 [2, 262144, 128], P('dp', 'morton'), may hold values from -6 to 6
- cot_node: bfloat16 [2, 65536, 128], P('dp', 'morton'), may hold values from -6 to 6
- cot_edge: bfloat16 [2, 262144, 128], P('dp', 'morton'), may hold values from -6 to 6
- senders: int32 [2, 262144], P('dp', 'morton'), may hold values from 0 to 767, as said below
- receivers: int32 [2, 262144], P('dp', 'morton'), may hold values from 0 to 511
- send_rows: int32 [2, 32768], P('dp', 'morton'), may hold values from 0 to 511
- edge_count: int32 [2, 128], P('dp', 'morton'), may hold values from 512 to 2048, as said below
- edge_w1: float32 [384, 128], replicated, may hold values from -0.3125 to 0.3125
- edge_w2: float32 [128, 128], replicated, may hold values from -0.5 to 0.5
- edge_gain: float32 [128], replicated, may hold values from 0.25 to 1.75
- node_w1: float32 [256, 128], replicated, may hold values from -0.375 to 0.375
- node_w2: float32 [128, 128], replicated, may hold values from -0.5 to 0.5
- node_gain: float32 [128], replicated, may hold values from 0.25 to 1.75
Outputs:
- grad_node: float32 [2, 65536, 128], P('dp', 'morton')
- grad_edge: float32 [2, 262144, 128], P('dp', 'morton')
- grad_edge_w1: float32 [384, 128], replicated
- grad_edge_w2: float32 [128, 128], replicated
- grad_edge_gain: float32 [128], replicated
- grad_node_w1: float32 [256, 128], replicated
- grad_node_w2: float32 [128, 128], replicated
- grad_node_gain: float32 [128], replicated
The draws below stay inside these ranges and needn't reach their ends.
Inputs may be any that keep to these rules, and one draw needn't show every extreme that they name: `senders`: on device m, an entry below 512 is one of its own cells; an entry 512 + k * 64 + q is ghost row q of group k, which comes from device m - d_k with d = (-128/2, -1, +1, +128/2); that device always exists. `send_rows`: entry k * 64 + q of device m is its local cell sent to device m + d_k, with d = (-128/2, -1, +1, +128/2). `edge_count`: edge slots at or beyond the count are empty; some device of every block is full.
All inputs are finite; a program needn't handle non-finite values.
Results may differ from the reference program's by a relative error of at most 0.014.
Values may be sent and summed in bfloat16 or wider, within the bound.
A program may use at most 64 MiB of HBM per device.

```python
import jax
import jax.numpy as jnp
from jax import lax

H = 128
C_DEV = 512
GQ = 64
E_DEV = 2048
BLOCKS = 2
CELLS = 65536
EDGES = 262144
N_MORTON = 128


def draw_senders(key, part):
    raw = jax.random.randint(key, (BLOCKS, EDGES), 0, C_DEV + 4 * GQ)
    device = (jnp.arange(EDGES) // E_DEV)[None, :]
    group = jnp.clip((raw - C_DEV) // GQ, 0, 3)
    offset = jnp.array([-(N_MORTON // 2), -1, 1, N_MORTON // 2], jnp.int32)[group]
    owner = device - offset
    wrong = (raw >= C_DEV) & ((owner < 0) | (owner >= N_MORTON))
    return jnp.where(wrong, raw % C_DEV, raw).astype(jnp.int32)


def draw_edge_count(key, part):
    counts = jax.random.randint(key, (BLOCKS, N_MORTON), E_DEV // 4, E_DEV + 1)
    fuller = jax.random.randint(jax.random.fold_in(key, 7), (BLOCKS,), 0, N_MORTON)
    chosen = jnp.arange(N_MORTON)[None, :] == fuller[:, None]
    return jnp.where(chosen, E_DEV, counts).astype(jnp.int32)


def touch_ends(values, key, low, top_value):
    shape = values.shape
    spot = [jax.random.randint(jax.random.fold_in(key, axis), (), 0, shape[axis]) for axis in range(len(shape))]
    values = values.at[tuple(spot)].set(low)
    longest = shape.index(max(shape))
    spot[longest] = (spot[longest] + 1) % shape[longest]
    return values.at[tuple(spot)].set(top_value)


def level_of(own_key, shape, split, low, largest):
    level = 1.0
    for position, blocks in split:
        steps = jax.random.uniform(jax.random.fold_in(jax.random.fold_in(own_key, 6), position), (blocks,), jnp.float32, low / len(split), largest / len(split))
        level = level * jnp.repeat(jnp.exp(steps), shape[position] // blocks).reshape((-1,) + (1,) * (len(shape) - 1 - position))
    return level


def scatter_about(key, extent, scale, reach, pieces=(), kind=jnp.bfloat16):
    values = scale * jax.random.normal(key, extent, jnp.float32)
    if pieces:
        values = values * level_of(key, extent, pieces, -0.22, 0.18)
    return jnp.clip(values, -reach, reach).astype(kind)


def setup_inputs(seed: int = 0) -> dict:
    keys = jax.random.split(jax.random.key(seed), 15)
    node_feat = scatter_about(keys[0], (BLOCKS, CELLS, H), 1.0, 6.0, ((0, 2), (1, 128)))
    edge_feat = scatter_about(keys[1], (BLOCKS, EDGES, H), 1.0, 6.0, ((0, 2), (1, 128)))
    cot_node = scatter_about(keys[2], (BLOCKS, CELLS, H), 1.0, 6.0, ((0, 2), (1, 128)))
    cot_edge = scatter_about(keys[3], (BLOCKS, EDGES, H), 1.0, 6.0, ((0, 2), (1, 128)))
    senders = draw_senders(jax.random.fold_in(keys[14], 71), 0)
    receivers = touch_ends(jax.random.randint(keys[5], (BLOCKS, EDGES), 0, C_DEV), jax.random.fold_in(keys[5], 1), 0, C_DEV - 1).astype(jnp.int32)
    send_rows = touch_ends(jax.random.randint(keys[6], (BLOCKS, N_MORTON * 4 * GQ), 0, C_DEV), jax.random.fold_in(keys[6], 1), 0, C_DEV - 1).astype(jnp.int32)
    edge_count = draw_edge_count(jax.random.fold_in(keys[14], 71), 0)
    edge_w1 = scatter_about(keys[8], (3 * H, H), (3 * H) ** -0.5, 0.3125, (), jnp.float32)
    edge_w2 = scatter_about(keys[9], (H, H), H ** -0.5, 0.5, (), jnp.float32)
    edge_gain = jnp.clip(1.0 + 0.15 * jax.random.normal(keys[10], (H,), jnp.float32), 0.25, 1.75)
    node_w1 = scatter_about(keys[11], (2 * H, H), (2 * H) ** -0.5, 0.375, (), jnp.float32)
    node_w2 = scatter_about(keys[12], (H, H), H ** -0.5, 0.5, (), jnp.float32)
    node_gain = jnp.clip(1.0 + 0.15 * jax.random.normal(keys[13], (H,), jnp.float32), 0.25, 1.75)
    return {"node_feat": node_feat, "edge_feat": edge_feat, "cot_node": cot_node, "cot_edge": cot_edge, "senders": senders, "receivers": receivers, "send_rows": send_rows, "edge_count": edge_count, "edge_w1": edge_w1, "edge_w2": edge_w2, "edge_gain": edge_gain, "node_w1": node_w1, "node_w2": node_w2, "node_gain": node_gain}


def layer_norm(values, gain):
    center = values - lax.optimization_barrier(jnp.mean(values, axis=-1, keepdims=True))
    spread = lax.optimization_barrier(jnp.mean(center * center, axis=-1, keepdims=True))
    return center * lax.rsqrt(spread + 1e-05) * gain

def local_forward(cells, ghosts, edges, ew1, ew2, egain, nw1, nw2, ngain, sending, receiving, count):
    table = jnp.concatenate([cells, ghosts], axis=0)
    joined = jnp.concatenate([edges.astype(jnp.bfloat16), table[sending].astype(jnp.bfloat16), cells[receiving].astype(jnp.bfloat16)], axis=1)
    first = jnp.dot(joined, ew1.astype(jnp.bfloat16), preferred_element_type=jnp.float32)
    second = jnp.dot(jax.nn.silu(first).astype(jnp.bfloat16), ew2.astype(jnp.bfloat16), preferred_element_type=jnp.float32)
    live = (jnp.arange(edges.shape[0]) < count).astype(edges.dtype)[:, None]
    edge_new = edges + live * layer_norm(second, egain)
    message = (live * edge_new).astype(jnp.bfloat16)
    gathered = jax.ops.segment_sum(message.astype(edges.dtype), receiving, num_segments=cells.shape[0])
    stacked = jnp.concatenate([cells.astype(jnp.bfloat16), gathered.astype(jnp.bfloat16)], axis=1)
    hidden = jnp.dot(stacked, nw1.astype(jnp.bfloat16), preferred_element_type=jnp.float32)
    output = jnp.dot(jax.nn.silu(hidden).astype(jnp.bfloat16), nw2.astype(jnp.bfloat16), preferred_element_type=jnp.float32)
    return (cells + layer_norm(output, ngain), edge_new)

def build_ghosts(cells_all, rows):
    offsets = (-(N_MORTON // 2), -1, 1, N_MORTON // 2)
    groups = []
    for k in range(4):
        shift_by = offsets[k]
        picked = jnp.take_along_axis(cells_all, rows[:, k, :, None], axis=1)
        blank = jnp.zeros((abs(shift_by),) + picked.shape[1:], cells_all.dtype)
        if shift_by > 0:
            moved = jnp.concatenate([blank, picked[:-shift_by]], axis=0)
        else:
            moved = jnp.concatenate([picked[-shift_by:], blank], axis=0)
        groups.append(moved)
    return jnp.concatenate(groups, axis=1)

def reference(node_feat, edge_feat, cot_node, cot_edge, senders, receivers, send_rows, edge_count, edge_w1, edge_w2, edge_gain, node_w1, node_w2, node_gain):
    weights = (edge_w1, edge_w2, edge_gain, node_w1, node_w2, node_gain)
    grad_nodes = []
    grad_edges = []
    totals = None
    for block in range(BLOCKS):
        cells_all = node_feat[block].astype(jnp.float32).reshape(N_MORTON, C_DEV, H)
        edges_all = edge_feat[block].astype(jnp.float32).reshape(N_MORTON, E_DEV, H)
        sending = senders[block].reshape(N_MORTON, E_DEV)
        receiving = receivers[block].reshape(N_MORTON, E_DEV)
        rows = send_rows[block].reshape(N_MORTON, 4, GQ)
        counts = edge_count[block]

        def whole(cells_all, edges_all, ew1, ew2, egain, nw1, nw2, ngain):
            ghosts = build_ghosts(cells_all, rows)

            def single(items):
                cells, ghost, edges, snd, rcv, cnt = items
                return local_forward(cells, ghost, edges, ew1, ew2, egain, nw1, nw2, ngain, snd, rcv, cnt)
            return lax.map(jax.checkpoint(single), (cells_all, ghosts, edges_all, sending, receiving, counts))
        outputs, pullback = jax.vjp(whole, cells_all, edges_all, *weights)
        cotangents = (cot_node[block].astype(jnp.float32).reshape(N_MORTON, C_DEV, H), cot_edge[block].astype(jnp.float32).reshape(N_MORTON, E_DEV, H))
        grads = pullback(cotangents)
        grad_nodes.append(grads[0].reshape(CELLS, H))
        grad_edges.append(grads[1].reshape(EDGES, H))
        if totals is None:
            totals = grads[2:]
        else:
            totals = tuple((a + b for a, b in zip(totals, grads[2:])))
    factor = 1.0 / jnp.sqrt(jnp.float32(BLOCKS * N_MORTON * E_DEV))
    scaled = tuple((t * factor for t in totals))
    return (jnp.stack(grad_nodes), jnp.stack(grad_edges), scaled[0], scaled[1], scaled[2], scaled[3], scaled[4], scaled[5])
```

```python
import functools

import jax
import jax.numpy as jnp
from jax import lax
from jax.experimental import pallas as pl
from jax.experimental.pallas import tpu as pltpu
from jax.sharding import PartitionSpec as P

MESH = pl.DeviceIdType.MESH
F32 = jnp.float32
BF16 = jnp.bfloat16
EDGE_TILE = 512


def nn(a, b):
    return lax.dot_general(a, b, (((1,), (0,)), ((), ())), preferred_element_type=F32)


def nt(a, b):
    return lax.dot_general(a, b, (((1,), (1,)), ((), ())), preferred_element_type=F32)


def one_hot(row, depth):
    spot = lax.broadcasted_iota(jnp.int32, (depth, row.shape[1]), 0)
    return jnp.where(spot == row, 1.0, 0.0).astype(BF16)


def sigmoid(a):
    return 0.5 * jnp.tanh(0.5 * a) + 0.5


def silu_parts(a):
    s = sigmoid(a)
    return a * s, s * (1.0 + a * (1.0 - s))


def column_of(row):
    return jnp.broadcast_to(row, (row.shape[1], row.shape[1])).T


def across(column, width):
    return jnp.concatenate([column] * (width // column.shape[1]), axis=1)


def folded(values):
    step = values.shape[0]
    return sum(values[:, i : i + step] for i in range(0, values.shape[1], step))


def row_of(partial):
    return jnp.sum(partial.T, axis=0, keepdims=True)


def normed(b):
    center = b - jnp.mean(b, axis=0, keepdims=True)
    spread = jnp.mean(center * center, axis=0, keepdims=True)
    rs = lax.rsqrt(spread + 1e-05)
    return center * rs, rs


def normed_back(dn, nh, rs):
    m1 = jnp.mean(dn, axis=0, keepdims=True)
    m2 = jnp.mean(dn * nh, axis=0, keepdims=True)
    return rs * (dn - m1 - nh * m2)


def kernel(
    sizes,
    node_hbm, edge_hbm, cotn_hbm, cote_hbm, snd, rcv, rows, cnt, w1, w2, eg, n1, n2, ng,
    gnode, gedge_hbm, gw1, gw2, geg, gn1, gn2, gng,
    h_v, e_v, cn_v, ce_v, in_sem,
    hot, tab, eT, a0, pT, dsil, nhat, rsv, daT, gT, gedge, out_sem,
    gs_send, gs_recv, gb_send, gb_recv, gsem_s, gsem_r, bsem_s, bsem_r,
    a_send, a_recv, b_send, b_recv, k_send, k_recv, zbuf, agbuf, psem_s, psem_r,
):
    peers, dps, plane, factor = sizes
    group = plane * dps
    depth = peers // plane
    C, H = h_v.shape
    E = e_v.shape[0]
    GH = rows.shape[1]
    GQ = GH // 4
    T = C + GH
    share = a_recv.shape[1]
    tiles = E // EDGE_TILE
    half = peers // 2
    last = group - 1

    m = lax.axis_index("morton")
    core = lax.axis_index("dp")
    level = m // plane
    mine = (m % plane) * dps + core
    low = m < half
    partner = lax.rem(m + half, peers)
    right = lax.rem(m + 1, peers)
    left = lax.rem(m + peers - 1, peers)

    def member(i):
        return (level * plane + i // dps, i % dps)

    def above(z):
        return (z * plane + m % plane, core)

    loads = [
        pltpu.make_async_copy(src, dst, in_sem.at[i])
        for i, (src, dst) in enumerate(((node_hbm, h_v), (edge_hbm, e_v), (cotn_hbm, cn_v), (cote_hbm, ce_v)))
    ]
    for load in loads:
        load.start()

    barrier = pltpu.get_barrier_semaphore()

    def greet(r, _):
        pl.semaphore_signal(barrier, inc=1, device_id=member(lax.rem(mine + r, group)), device_id_type=MESH)
        return 0

    lax.fori_loop(1, group, greet, 0)

    def greet_above(r, _):
        pl.semaphore_signal(barrier, inc=1, device_id=above(lax.rem(level + r, depth)), device_id_type=MESH)
        return 0

    lax.fori_loop(1, depth, greet_above, 0)
    for side in (left, right):
        pl.semaphore_signal(barrier, inc=1, device_id=(side, core), device_id_type=MESH)

    eye_r = lax.broadcasted_iota(jnp.int32, (H, H), 0)
    eye_c = lax.broadcasted_iota(jnp.int32, (H, H), 1)
    eye = jnp.where(eye_r == eye_c, 1.0, 0.0).astype(BF16)

    lane = lax.broadcasted_iota(jnp.int32, (1, GH), 1)
    first_used = jnp.logical_and(lane < GQ, jnp.logical_not(low))
    last_used = jnp.logical_and(lane >= 3 * GQ, low)
    middle = jnp.logical_and(lane >= GQ, lane < 3 * GQ)
    used = jnp.logical_or(middle, jnp.logical_or(first_used, last_used))
    hot_out = one_hot(jnp.where(used, rows[...], -1), C)

    loads[0].wait()
    hT = nt(eye, h_v[...]).astype(BF16)
    tab[:, 0:C] = hT
    picked = nn(hT, hot_out).T
    gs_send[0] = (picked[0:GQ] + picked[3 * GQ : 4 * GQ]).astype(BF16)
    gs_send[1] = picked[GQ : 2 * GQ].astype(BF16)
    gs_send[2] = picked[2 * GQ : 3 * GQ].astype(BF16)

    pl.semaphore_wait(barrier, (group - 1) + (depth - 1) + 2)

    ghost_out = [
        pltpu.make_async_remote_copy(
            src_ref=gs_send.at[k], dst_ref=gs_recv.at[k], send_sem=gsem_s.at[k], recv_sem=gsem_r.at[k],
            device_id=(to, core), device_id_type=MESH,
        )
        for k, to in enumerate((partner, left, right))
    ]
    for copy in ghost_out:
        copy.start()

    w1T = nt(eye, w1[...].astype(BF16)).astype(BF16)
    w2T = nt(eye, w2[...].astype(BF16)).astype(BF16)
    w1s_T = w1T[:, H : 2 * H]
    loads[1].wait()

    def ahead(i, _):
        cols = pl.ds(pl.multiple_of(i * EDGE_TILE, EDGE_TILE), EDGE_TILE)
        hot_s = one_hot(snd[:, cols], T)
        hot_r = one_hot(rcv[:, cols], C)
        hot[0:T, cols] = hot_s
        hot[T : T + C, cols] = hot_r
        et = nt(eye, e_v[cols, :]).astype(BF16)
        eT[:, cols] = et
        xs = nn(hT, hot_s[0:C]).astype(BF16)
        xr = nn(hT, hot_r).astype(BF16)
        a0[:, cols] = nn(w1T, jnp.concatenate([et, xs, xr], axis=0))
        return 0

    lax.fori_loop(0, tiles, ahead, 0)

    gain_e = column_of(eg[...])
    gain_n = column_of(ng[...])
    gain_tile = across(gain_e, EDGE_TILE)
    count = cnt[0, 0]

    for copy in ghost_out:
        copy.wait_recv()
    ghosts = jnp.concatenate([gs_recv[0], gs_recv[1], gs_recv[2], gs_recv[0]], axis=0)
    first_here = jnp.logical_and(lane < GQ, low)
    last_here = jnp.logical_and(lane >= 3 * GQ, jnp.logical_not(low))
    here = jnp.logical_or(middle, jnp.logical_or(first_here, last_here))
    ghost_T = jnp.where(here, nt(eye, ghosts), 0.0).astype(BF16)
    tab[:, C:T] = ghost_T

    def live_row(i):
        slot = lax.broadcasted_iota(jnp.int32, (1, EDGE_TILE), 1) + i * EDGE_TILE
        return jnp.where(slot < count, 1.0, 0.0)

    def forward(i, agg):
        cols = pl.ds(pl.multiple_of(i * EDGE_TILE, EDGE_TILE), EDGE_TILE)
        xg = nn(ghost_T, hot[C:T, cols]).astype(BF16)
        a = a0[:, cols] + nn(w1s_T, xg)
        p, d = silu_parts(a)
        p = p.astype(BF16)
        pT[:, cols] = p
        dsil[:, cols] = d
        nh, rs = normed(nn(w2T, p))
        nhat[:, cols] = nh
        rsv[:, cols] = rs
        live = live_row(i)
        msg = (live * (eT[:, cols].astype(F32) + live * (nh * gain_tile))).astype(BF16)
        return agg + nt(msg, hot[T : T + C, cols])

    agg = lax.fori_loop(0, tiles, forward, jnp.zeros((H, C), F32)).astype(BF16)

    n1b = n1[...].astype(BF16)
    n2b = n2[...].astype(BF16)
    n1T = nt(eye, n1b).astype(BF16)
    n2T = nt(eye, n2b).astype(BF16)
    loads[2].wait()
    yT = jnp.concatenate([hT, agg], axis=0)
    r, dr_ = silu_parts(nn(n1T, yT))
    r = r.astype(BF16)
    nh, rs = normed(nn(n2T, r))
    cnT = nt(eye, cn_v[...])
    acc = folded(cnT * nh)
    ds = normed_back(cnT * across(gain_n, C), nh, rs).astype(BF16)
    dc = (nn(n2b, ds).astype(BF16).astype(F32) * dr_).astype(BF16)
    dyT = nn(n1b, dc).astype(BF16)
    dagg = dyT[H:]
    b_send[0 : 2 * H] = nt(yT, dc).astype(BF16)
    b_send[2 * H : 3 * H] = nt(r, ds).astype(BF16)
    b_send[3 * H :] = jnp.zeros((b_send.shape[0] - 3 * H, H), BF16)
    gain_n_row = row_of(acc)
    node_T = cnT + dyT[0:H].astype(F32)

    def shard(i):
        return pl.ds(pl.multiple_of(i * share, share), share)

    def spread(src, dst, phase):
        def go(r, _):
            i = lax.rem(mine + r, group)
            pltpu.make_async_remote_copy(
                src_ref=src.at[shard(i)], dst_ref=dst.at[mine], send_sem=psem_s.at[phase], recv_sem=psem_r.at[phase],
                device_id=member(i), device_id_type=MESH,
            ).start()
            return 0

        lax.fori_loop(1, group, go, 0)

    def all_arrived(dst, phase, sems):
        several = dst.at[pl.ds(0, dst.shape[0] - 1)]
        pltpu.make_async_copy(several, several, sems.at[phase]).wait()

    spread(b_send, b_recv, 0)
    b_recv[mine] = b_send[shard(mine)]

    loads[3].wait()
    w2b = w2[...].astype(BF16)

    def backward(i, acc):
        cols = pl.ds(pl.multiple_of(i * EDGE_TILE, EDGE_TILE), EDGE_TILE)
        live = live_row(i)
        g = nt(eye, ce_v[cols, :]) + live * nn(dagg, hot[T : T + C, cols])
        gT[:, cols] = g
        dd = live * g
        nh = nhat[:, cols]
        acc = acc + folded(dd * nh)
        db = normed_back(dd * gain_tile, nh, rsv[:, cols]).astype(BF16)
        dp = nn(w2b, db).astype(BF16).astype(F32)
        daT[:, cols] = (dp * dsil[:, cols]).astype(BF16)
        return acc, db

    def backward_step(i, carry):
        acc, dw2 = carry
        cols = pl.ds(pl.multiple_of(i * EDGE_TILE, EDGE_TILE), EDGE_TILE)
        acc, db = backward(i, acc)
        return acc, dw2 + nt(pT[:, cols], db)

    acc, dw2 = lax.fori_loop(0, tiles, backward_step, (jnp.zeros((H, H), F32), jnp.zeros((H, H), F32)))

    da = daT[...]
    s_all = nt(hot[...], da).astype(BF16)
    a_send[0:H] = nt(eT[...], da).astype(BF16)
    a_send[H : 2 * H] = nn(tab[...], s_all[0:T]).astype(BF16)
    a_send[2 * H : 3 * H] = nn(hT, s_all[T:]).astype(BF16)
    a_send[3 * H :] = dw2.astype(BF16)
    k_send[...] = jnp.zeros_like(k_send)
    k_send[0:1] = row_of(acc).astype(BF16)
    k_send[1:2] = gain_n_row.astype(BF16)

    spread(a_send, a_recv, 1)
    a_recv[mine] = a_send[shard(mine)]

    to_last = pltpu.make_async_remote_copy(
        src_ref=k_send, dst_ref=k_recv.at[mine], send_sem=psem_s.at[2], recv_sem=psem_r.at[2],
        device_id=member(last), device_id_type=MESH,
    )

    @pl.when(mine != last)
    def _():
        to_last.start()

    w1b = w1[...].astype(BF16)
    dghost = nt(s_all[C:T], w1b[H : 2 * H])
    gb_send[0] = (dghost[0:GQ] + dghost[3 * GQ : 4 * GQ]).astype(BF16)
    gb_send[1] = dghost[GQ : 2 * GQ].astype(BF16)
    gb_send[2] = dghost[2 * GQ : 3 * GQ].astype(BF16)
    ghost_back = [
        pltpu.make_async_remote_copy(
            src_ref=gb_send.at[k], dst_ref=gb_recv.at[k], send_sem=bsem_s.at[k], recv_sem=bsem_r.at[k],
            device_id=(to, core), device_id_type=MESH,
        )
        for k, to in enumerate((partner, right, left))
    ]
    for copy in ghost_back:
        copy.start()

    def edge_out(i, _):
        cols = pl.ds(pl.multiple_of(i * EDGE_TILE, EDGE_TILE), EDGE_TILE)
        dx = nn(w1b[0:H], daT[:, cols]).astype(BF16).astype(F32)
        gedge[cols, :] = (gT[:, cols] + dx).T
        return 0

    def edge_store(i):
        cols = pl.ds(i * EDGE_TILE, EDGE_TILE)
        return pltpu.make_async_copy(gedge.at[cols], gedge_hbm.at[cols], out_sem.at[i])

    lax.fori_loop(0, tiles // 2, edge_out, 0)
    for i in range(tiles // 2):
        edge_store(i).start()

    all_arrived(a_recv, 1, psem_r)
    all_arrived(b_recv, 0, psem_r)
    zbuf[level, 0:share] = jnp.sum(a_recv[...].astype(F32), axis=0).astype(BF16)

    @pl.when(mine == last)
    def _():
        k_recv[mine] = k_send[...]
        all_arrived(k_recv, 2, psem_r)
        total = jnp.sum(k_recv[:, 0:16].astype(F32), axis=0).astype(BF16)
        zbuf[level, share : 2 * share] = jnp.zeros((share, H), BF16)
        zbuf[level, share : share + 16] = total

    @pl.when(mine != last)
    def _():
        zbuf[level, share : 2 * share] = jnp.sum(b_recv[...].astype(F32), axis=0).astype(BF16)

    def climb(r, _):
        pltpu.make_async_remote_copy(
            src_ref=zbuf.at[level], dst_ref=zbuf.at[level], send_sem=psem_s.at[3], recv_sem=psem_r.at[3],
            device_id=above(lax.rem(level + r, depth)), device_id_type=MESH,
        ).start()
        return 0

    lax.fori_loop(1, depth, climb, 0)

    lax.fori_loop(tiles // 2, tiles, edge_out, 0)
    for i in range(tiles // 2, tiles):
        edge_store(i).start()

    all_arrived(zbuf, 3, psem_r)
    agbuf[mine] = (jnp.sum(zbuf[...].astype(F32), axis=0) * factor).astype(BF16)

    def share_out(r, _):
        pltpu.make_async_remote_copy(
            src_ref=agbuf.at[mine], dst_ref=agbuf.at[mine], send_sem=psem_s.at[4], recv_sem=psem_r.at[4],
            device_id=member(lax.rem(mine + r, group)), device_id_type=MESH,
        ).start()
        return 0

    lax.fori_loop(1, group, share_out, 0)

    own = nt(s_all[0:C], w1b[H : 2 * H]).astype(BF16).astype(F32)
    own = own + nt(s_all[T:], w1b[2 * H : 3 * H]).astype(BF16).astype(F32)
    for copy in ghost_back:
        copy.wait_recv()
    back = jnp.concatenate([gb_recv[0], gb_recv[1], gb_recv[2], gb_recv[0]], axis=0)
    gnode[...] = node_T.T + own + nn(hot_out, back)

    all_arrived(agbuf, 4, psem_r)

    def landed(start, stop, offset):
        count = (stop - start) // share
        part = agbuf[start // share : start // share + count, offset : offset + share]
        return part.astype(F32).reshape(stop - start, H)

    gw1[...] = landed(0, 3 * H, 0)
    gw2[...] = landed(3 * H, 4 * H, 0)
    gn1[...] = landed(0, 2 * H, share)
    gn2[...] = landed(2 * H, 3 * H, share)
    tail = agbuf[last, share : share + 16].astype(F32)
    geg[...] = tail[0:1]
    gng[...] = tail[1:2]

    for copy in ghost_out + ghost_back:
        copy.wait_send()
    all_arrived(b_recv, 0, psem_s)
    all_arrived(a_recv, 1, psem_s)
    all_arrived(zbuf, 3, psem_s)
    all_arrived(agbuf, 4, psem_s)

    @pl.when(mine != last)
    def _():
        to_last.wait_send()

    for i in range(tiles):
        edge_store(i).wait()


def on_device(
    plane, node_feat, edge_feat, cot_node, cot_edge, senders, receivers, send_rows, edge_count,
    edge_w1, edge_w2, edge_gain, node_w1, node_w2, node_gain,
):
    peers, dps = lax.axis_size("morton"), lax.axis_size("dp")
    C, H = node_feat.shape[1:]
    E = edge_feat.shape[1]
    GH = send_rows.shape[1]
    GQ = GH // 4
    T = C + GH
    group = plane * dps
    depth = peers // plane
    share = 4 * H // group
    factor = (dps * peers * E) ** -0.5
    vmem = pl.BlockSpec(memory_space=pltpu.VMEM)
    smem = pl.BlockSpec(memory_space=pltpu.SMEM)
    hbm = pl.BlockSpec(memory_space=pl.ANY)
    shape = jax.ShapeDtypeStruct
    dma = pltpu.SemaphoreType.DMA
    tiles = E // EDGE_TILE
    outs = pl.pallas_call(
        functools.partial(kernel, (peers, dps, plane, factor)),
        out_shape=[
            shape((C, H), F32), shape((E, H), F32), shape((3 * H, H), F32), shape((H, H), F32),
            shape((1, H), F32), shape((2 * H, H), F32), shape((H, H), F32), shape((1, H), F32),
        ],
        in_specs=[hbm, hbm, hbm, hbm, vmem, vmem, vmem, smem] + [vmem] * 6,
        out_specs=[vmem, hbm] + [vmem] * 6,
        scratch_shapes=[
            pltpu.VMEM((C, H), BF16), pltpu.VMEM((E, H), BF16), pltpu.VMEM((C, H), BF16), pltpu.VMEM((E, H), BF16),
            dma((4,)),
            pltpu.VMEM((T + C, E), BF16), pltpu.VMEM((H, T), BF16), pltpu.VMEM((H, E), BF16),
            pltpu.VMEM((H, E), F32), pltpu.VMEM((H, E), BF16), pltpu.VMEM((H, E), F32), pltpu.VMEM((H, E), F32),
            pltpu.VMEM((1, E), F32), pltpu.VMEM((H, E), BF16), pltpu.VMEM((H, E), F32), pltpu.VMEM((E, H), F32),
            dma((tiles,)),
            pltpu.VMEM((3, GQ, H), BF16), pltpu.VMEM((3, GQ, H), BF16),
            pltpu.VMEM((3, GQ, H), BF16), pltpu.VMEM((3, GQ, H), BF16),
            dma((3,)), dma((3,)), dma((3,)), dma((3,)),
            pltpu.VMEM((4 * H, H), BF16), pltpu.VMEM((group, share, H), BF16),
            pltpu.VMEM((4 * H, H), BF16), pltpu.VMEM((group, share, H), BF16),
            pltpu.VMEM((16, H), BF16), pltpu.VMEM((group, 16, H), BF16),
            pltpu.VMEM((depth, 2 * share, H), BF16), pltpu.VMEM((group, 2 * share, H), BF16),
            dma((5,)), dma((5,)),
        ],
        compiler_params=pltpu.CompilerParams(
            collective_id=0, has_side_effects=True, vmem_limit_bytes=40 * 1024 * 1024
        ),
    )(
        node_feat[0], edge_feat[0], cot_node[0], cot_edge[0], senders, receivers, send_rows, edge_count,
        edge_w1, edge_w2, edge_gain.reshape(1, H), node_w1, node_w2, node_gain.reshape(1, H),
    )
    return (
        outs[0][None], outs[1][None], outs[2], outs[3], outs[4].reshape(H), outs[5], outs[6], outs[7].reshape(H)
    )


def solution(mesh):
    cells = P("dp", "morton", None)
    flat = P("dp", "morton")
    plane = min(16, mesh.shape["morton"] // 2)
    return jax.shard_map(
        functools.partial(on_device, plane),
        mesh=mesh,
        in_specs=(cells, cells, cells, cells, flat, flat, flat, flat, P(), P(), P(), P(), P(), P()),
        out_specs=(cells, cells, P(), P(), P(), P(), P(), P()),
        check_vma=False,
    )
```

```python
import functools

import jax
import jax.numpy as jnp
from jax import lax
from jax.experimental import pallas as pl
from jax.experimental.pallas import tpu as pltpu
from jax.sharding import PartitionSpec as P

MESH = pl.DeviceIdType.MESH
F32 = jnp.float32
BF16 = jnp.bfloat16
EDGE_TILE = 512


def nn(a, b):
    return lax.dot_general(a, b, (((1,), (0,)), ((), ())), preferred_element_type=F32)


def nt(a, b):
    return lax.dot_general(a, b, (((1,), (1,)), ((), ())), preferred_element_type=F32)


def one_hot(row, depth):
    spot = lax.broadcasted_iota(jnp.int32, (depth, row.shape[1]), 0)
    return jnp.where(spot == row, 1.0, 0.0).astype(BF16)


def sigmoid(a):
    return 0.5 * jnp.tanh(0.5 * a) + 0.5


def silu_parts(a):
    s = sigmoid(a)
    return a * s, s * (1.0 + a * (1.0 - s))


def column_of(row):
    return jnp.broadcast_to(row, (row.shape[1], row.shape[1])).T


def across(column, width):
    return jnp.concatenate([column] * (width // column.shape[1]), axis=1)


def folded(values):
    step = values.shape[0]
    return sum(values[:, i : i + step] for i in range(0, values.shape[1], step))


def row_of(partial):
    return jnp.sum(partial.T, axis=0, keepdims=True)


def normed(b):
    center = b - jnp.mean(b, axis=0, keepdims=True)
    spread = jnp.mean(center * center, axis=0, keepdims=True)
    rs = lax.rsqrt(spread + 1e-05)
    return center * rs, rs


def normed_back(dn, nh, rs):
    m1 = jnp.mean(dn, axis=0, keepdims=True)
    m2 = jnp.mean(dn * nh, axis=0, keepdims=True)
    return rs * (dn - m1 - nh * m2)


def kernel(
    sizes,
    node_hbm, rows_hbm, edge_hbm, snd_hbm, rcv_hbm, w1_hbm, w2_hbm, cnt_hbm,
    eg_hbm, ng_hbm, n1_hbm, n2_hbm, cotn_hbm, cote_hbm,
    gnode, gedge, gw1, gw2, geg, gn1, gn2, gng,
    h_v, rows, e_v, snd, rcv, w1, w2, cnt, eg, ng, n1, n2, cn_v, ce_v, in_sem,
    hot, tab, eT, a0, pT, dsil, nhat, rsv, daT, gT,
    gs_send, gs_recv, gb_send, gb_recv, gsem_s, gsem_r, bsem_s, bsem_r,
    a_send, a_recv, b_send, b_recv, k_send, k_recv, zbuf, agbuf, psem_s, psem_r,
):
    peers, dps, plane, factor = sizes
    group = plane * dps
    depth = peers // plane
    C, H = h_v.shape
    E = e_v.shape[0]
    GH = rows.shape[1]
    GQ = GH // 4
    T = C + GH
    share = a_recv.shape[1]
    tiles = E // EDGE_TILE
    half = peers // 2
    last = group - 1

    m = lax.axis_index("morton")
    core = lax.axis_index("dp")
    level = m // plane
    mine = (m % plane) * dps + core
    low = m < half
    partner = lax.rem(m + half, peers)
    right = lax.rem(m + 1, peers)
    left = lax.rem(m + peers - 1, peers)

    def member(i):
        return (level * plane + i // dps, i % dps)

    def above(z):
        return (z * plane + m % plane, core)

    sources = (
        node_hbm, rows_hbm, edge_hbm, snd_hbm, rcv_hbm, w1_hbm, w2_hbm, cnt_hbm,
        eg_hbm, ng_hbm, n1_hbm, n2_hbm, cotn_hbm, cote_hbm,
    )
    places = (h_v, rows, e_v, snd, rcv, w1, w2, cnt, eg, ng, n1, n2, cn_v, ce_v)
    loads = [
        pltpu.make_async_copy(src, dst, in_sem.at[i]) for i, (src, dst) in enumerate(zip(sources, places))
    ]
    for load in loads:
        load.start()

    barrier = pltpu.get_barrier_semaphore()

    def greet(r, _):
        pl.semaphore_signal(barrier, inc=1, device_id=member(lax.rem(mine + r, group)), device_id_type=MESH)
        return 0

    lax.fori_loop(1, group, greet, 0)

    def greet_above(r, _):
        pl.semaphore_signal(barrier, inc=1, device_id=above(lax.rem(level + r, depth)), device_id_type=MESH)
        return 0

    lax.fori_loop(1, depth, greet_above, 0)
    for side in (left, right):
        pl.semaphore_signal(barrier, inc=1, device_id=(side, core), device_id_type=MESH)

    eye_r = lax.broadcasted_iota(jnp.int32, (H, H), 0)
    eye_c = lax.broadcasted_iota(jnp.int32, (H, H), 1)
    eye = jnp.where(eye_r == eye_c, 1.0, 0.0).astype(BF16)

    lane = lax.broadcasted_iota(jnp.int32, (1, GH), 1)
    first_used = jnp.logical_and(lane < GQ, jnp.logical_not(low))
    last_used = jnp.logical_and(lane >= 3 * GQ, low)
    middle = jnp.logical_and(lane >= GQ, lane < 3 * GQ)
    used = jnp.logical_or(middle, jnp.logical_or(first_used, last_used))
    loads[0].wait()
    loads[1].wait()
    hot_out = one_hot(jnp.where(used, rows[...], -1), C)

    hT = nt(eye, h_v[...]).astype(BF16)
    tab[:, 0:C] = hT
    picked = nn(hT, hot_out).T
    gs_send[0] = (picked[0:GQ] + picked[3 * GQ : 4 * GQ]).astype(BF16)
    gs_send[1] = picked[GQ : 2 * GQ].astype(BF16)
    gs_send[2] = picked[2 * GQ : 3 * GQ].astype(BF16)

    pl.semaphore_wait(barrier, (group - 1) + (depth - 1) + 2)

    ghost_out = [
        pltpu.make_async_remote_copy(
            src_ref=gs_send.at[k], dst_ref=gs_recv.at[k], send_sem=gsem_s.at[k], recv_sem=gsem_r.at[k],
            device_id=(to, core), device_id_type=MESH,
        )
        for k, to in enumerate((partner, left, right))
    ]
    for copy in ghost_out:
        copy.start()

    for load in loads[2:7]:
        load.wait()
    w1T = nt(eye, w1[...].astype(BF16)).astype(BF16)
    w2T = nt(eye, w2[...].astype(BF16)).astype(BF16)
    w1s_T = w1T[:, H : 2 * H]

    def ahead(i, _):
        cols = pl.ds(pl.multiple_of(i * EDGE_TILE, EDGE_TILE), EDGE_TILE)
        hot_s = one_hot(snd[:, cols], T)
        hot_r = one_hot(rcv[:, cols], C)
        hot[0:T, cols] = hot_s
        hot[T : T + C, cols] = hot_r
        et = nt(eye, e_v[cols, :]).astype(BF16)
        eT[:, cols] = et
        xs = nn(hT, hot_s[0:C]).astype(BF16)
        xr = nn(hT, hot_r).astype(BF16)
        a0[:, cols] = nn(w1T, jnp.concatenate([et, xs, xr], axis=0))
        return 0

    lax.fori_loop(0, tiles, ahead, 0)

    for load in loads[7:12]:
        load.wait()
    gain_e = column_of(eg[...])
    gain_n = column_of(ng[...])
    gain_tile = across(gain_e, EDGE_TILE)
    count = cnt[0, 0]

    for copy in ghost_out:
        copy.wait_recv()
    ghosts = jnp.concatenate([gs_recv[0], gs_recv[1], gs_recv[2], gs_recv[0]], axis=0)
    first_here = jnp.logical_and(lane < GQ, low)
    last_here = jnp.logical_and(lane >= 3 * GQ, jnp.logical_not(low))
    here = jnp.logical_or(middle, jnp.logical_or(first_here, last_here))
    ghost_T = jnp.where(here, nt(eye, ghosts), 0.0).astype(BF16)
    tab[:, C:T] = ghost_T

    def live_row(i):
        slot = lax.broadcasted_iota(jnp.int32, (1, EDGE_TILE), 1) + i * EDGE_TILE
        return jnp.where(slot < count, 1.0, 0.0)

    def forward(i, agg):
        cols = pl.ds(pl.multiple_of(i * EDGE_TILE, EDGE_TILE), EDGE_TILE)
        xg = nn(ghost_T, hot[C:T, cols]).astype(BF16)
        a = a0[:, cols] + nn(w1s_T, xg)
        p, d = silu_parts(a)
        p = p.astype(BF16)
        pT[:, cols] = p
        dsil[:, cols] = d
        nh, rs = normed(nn(w2T, p))
        nhat[:, cols] = nh
        rsv[:, cols] = rs
        live = live_row(i)
        msg = (live * (eT[:, cols].astype(F32) + live * (nh * gain_tile))).astype(BF16)
        return agg + nt(msg, hot[T : T + C, cols])

    agg = lax.fori_loop(0, tiles, forward, jnp.zeros((H, C), F32)).astype(BF16)

    n1b = n1[...].astype(BF16)
    n2b = n2[...].astype(BF16)
    n1T = nt(eye, n1b).astype(BF16)
    n2T = nt(eye, n2b).astype(BF16)
    loads[12].wait()
    yT = jnp.concatenate([hT, agg], axis=0)
    r, dr_ = silu_parts(nn(n1T, yT))
    r = r.astype(BF16)
    nh, rs = normed(nn(n2T, r))
    cnT = nt(eye, cn_v[...])
    acc = folded(cnT * nh)
    ds = normed_back(cnT * across(gain_n, C), nh, rs).astype(BF16)
    dc = (nn(n2b, ds).astype(BF16).astype(F32) * dr_).astype(BF16)
    dyT = nn(n1b, dc).astype(BF16)
    dagg = dyT[H:]
    b_send[0 : 2 * H] = nt(yT, dc).astype(BF16)
    b_send[2 * H : 3 * H] = nt(r, ds).astype(BF16)
    b_send[3 * H :] = jnp.zeros((b_send.shape[0] - 3 * H, H), BF16)
    gain_n_row = row_of(acc)
    node_T = cnT + dyT[0:H].astype(F32)

    def shard(i):
        return pl.ds(pl.multiple_of(i * share, share), share)

    def spread(src, dst, phase):
        def go(r, _):
            i = lax.rem(mine + r, group)
            pltpu.make_async_remote_copy(
                src_ref=src.at[shard(i)], dst_ref=dst.at[mine], send_sem=psem_s.at[phase], recv_sem=psem_r.at[phase],
                device_id=member(i), device_id_type=MESH,
            ).start()
            return 0

        lax.fori_loop(1, group, go, 0)

    def all_arrived(dst, phase, sems):
        several = dst.at[pl.ds(0, dst.shape[0] - 1)]
        pltpu.make_async_copy(several, several, sems.at[phase]).wait()

    spread(b_send, b_recv, 0)
    b_recv[mine] = b_send[shard(mine)]

    loads[13].wait()
    w2b = w2[...].astype(BF16)

    def backward(i, acc):
        cols = pl.ds(pl.multiple_of(i * EDGE_TILE, EDGE_TILE), EDGE_TILE)
        live = live_row(i)
        g = nt(eye, ce_v[cols, :]) + live * nn(dagg, hot[T : T + C, cols])
        gT[:, cols] = g
        dd = live * g
        nh = nhat[:, cols]
        acc = acc + folded(dd * nh)
        db = normed_back(dd * gain_tile, nh, rsv[:, cols]).astype(BF16)
        dp = nn(w2b, db).astype(BF16).astype(F32)
        daT[:, cols] = (dp * dsil[:, cols]).astype(BF16)
        return acc, db

    def backward_step(i, carry):
        acc, dw2 = carry
        cols = pl.ds(pl.multiple_of(i * EDGE_TILE, EDGE_TILE), EDGE_TILE)
        acc, db = backward(i, acc)
        return acc, dw2 + nt(pT[:, cols], db)

    acc, dw2 = lax.fori_loop(0, tiles, backward_step, (jnp.zeros((H, H), F32), jnp.zeros((H, H), F32)))

    da = daT[...]
    s_all = nt(hot[...], da).astype(BF16)
    a_send[0:H] = nt(eT[...], da).astype(BF16)
    a_send[H : 2 * H] = nn(tab[...], s_all[0:T]).astype(BF16)
    a_send[2 * H : 3 * H] = nn(hT, s_all[T:]).astype(BF16)
    a_send[3 * H :] = dw2.astype(BF16)
    k_send[...] = jnp.zeros_like(k_send)
    k_send[0:1] = row_of(acc).astype(BF16)
    k_send[1:2] = gain_n_row.astype(BF16)

    spread(a_send, a_recv, 1)
    a_recv[mine] = a_send[shard(mine)]

    to_last = pltpu.make_async_remote_copy(
        src_ref=k_send, dst_ref=k_recv.at[mine], send_sem=psem_s.at[2], recv_sem=psem_r.at[2],
        device_id=member(last), device_id_type=MESH,
    )

    @pl.when(mine != last)
    def _():
        to_last.start()

    w1b = w1[...].astype(BF16)
    dghost = nt(s_all[C:T], w1b[H : 2 * H])
    gb_send[0] = (dghost[0:GQ] + dghost[3 * GQ : 4 * GQ]).astype(BF16)
    gb_send[1] = dghost[GQ : 2 * GQ].astype(BF16)
    gb_send[2] = dghost[2 * GQ : 3 * GQ].astype(BF16)
    ghost_back = [
        pltpu.make_async_remote_copy(
            src_ref=gb_send.at[k], dst_ref=gb_recv.at[k], send_sem=bsem_s.at[k], recv_sem=bsem_r.at[k],
            device_id=(to, core), device_id_type=MESH,
        )
        for k, to in enumerate((partner, right, left))
    ]
    for copy in ghost_back:
        copy.start()

    def edge_out(i, _):
        cols = pl.ds(pl.multiple_of(i * EDGE_TILE, EDGE_TILE), EDGE_TILE)
        dx = nn(w1b[0:H], daT[:, cols]).astype(BF16).astype(F32)
        gedge[cols, :] = (gT[:, cols] + dx).T
        return 0

    lax.fori_loop(0, tiles // 2, edge_out, 0)

    all_arrived(a_recv, 1, psem_r)
    all_arrived(b_recv, 0, psem_r)
    zbuf[level, 0:share] = jnp.sum(a_recv[...].astype(F32), axis=0).astype(BF16)

    @pl.when(mine == last)
    def _():
        k_recv[mine] = k_send[...]
        all_arrived(k_recv, 2, psem_r)
        total = jnp.sum(k_recv[:, 0:16].astype(F32), axis=0).astype(BF16)
        zbuf[level, share : 2 * share] = jnp.zeros((share, H), BF16)
        zbuf[level, share : share + 16] = total

    @pl.when(mine != last)
    def _():
        zbuf[level, share : 2 * share] = jnp.sum(b_recv[...].astype(F32), axis=0).astype(BF16)

    def climb(r, _):
        pltpu.make_async_remote_copy(
            src_ref=zbuf.at[level], dst_ref=zbuf.at[level], send_sem=psem_s.at[3], recv_sem=psem_r.at[3],
            device_id=above(lax.rem(level + r, depth)), device_id_type=MESH,
        ).start()
        return 0

    lax.fori_loop(1, depth, climb, 0)

    lax.fori_loop(tiles // 2, tiles, edge_out, 0)

    all_arrived(zbuf, 3, psem_r)
    agbuf[mine] = (jnp.sum(zbuf[...].astype(F32), axis=0) * factor).astype(BF16)

    def share_out(r, _):
        pltpu.make_async_remote_copy(
            src_ref=agbuf.at[mine], dst_ref=agbuf.at[mine], send_sem=psem_s.at[4], recv_sem=psem_r.at[4],
            device_id=member(lax.rem(mine + r, group)), device_id_type=MESH,
        ).start()
        return 0

    lax.fori_loop(1, group, share_out, 0)

    own = nt(s_all[0:C], w1b[H : 2 * H]).astype(BF16).astype(F32)
    own = own + nt(s_all[T:], w1b[2 * H : 3 * H]).astype(BF16).astype(F32)
    for copy in ghost_back:
        copy.wait_recv()
    back = jnp.concatenate([gb_recv[0], gb_recv[1], gb_recv[2], gb_recv[0]], axis=0)
    gnode[...] = node_T.T + own + nn(hot_out, back)

    all_arrived(agbuf, 4, psem_r)

    def landed(start, stop, offset):
        count = (stop - start) // share
        part = agbuf[start // share : start // share + count, offset : offset + share]
        return part.astype(F32).reshape(stop - start, H)

    gw1[...] = landed(0, 3 * H, 0)
    gw2[...] = landed(3 * H, 4 * H, 0)
    gn1[...] = landed(0, 2 * H, share)
    gn2[...] = landed(2 * H, 3 * H, share)
    tail = agbuf[last, share : share + 16].astype(F32)
    geg[...] = tail[0:1]
    gng[...] = tail[1:2]

    for copy in ghost_out + ghost_back:
        copy.wait_send()
    all_arrived(b_recv, 0, psem_s)
    all_arrived(a_recv, 1, psem_s)
    all_arrived(zbuf, 3, psem_s)
    all_arrived(agbuf, 4, psem_s)

    @pl.when(mine != last)
    def _():
        to_last.wait_send()


def deliver(*refs):
    n = len(refs) // 2
    sem = refs[-1]
    copies = [pltpu.make_async_copy(refs[i], refs[n + i], sem.at[i]) for i in range(n)]
    for copy in copies:
        copy.start()
    for copy in copies:
        copy.wait()


def on_device(
    plane, node_feat, edge_feat, cot_node, cot_edge, senders, receivers, send_rows, edge_count,
    edge_w1, edge_w2, edge_gain, node_w1, node_w2, node_gain,
):
    peers, dps = lax.axis_size("morton"), lax.axis_size("dp")
    C, H = node_feat.shape[1:]
    E = edge_feat.shape[1]
    GH = send_rows.shape[1]
    GQ = GH // 4
    T = C + GH
    group = plane * dps
    depth = peers // plane
    share = 4 * H // group
    factor = (dps * peers * E) ** -0.5
    vmem = pl.BlockSpec(memory_space=pltpu.VMEM)
    hbm = pl.BlockSpec(memory_space=pltpu.HBM)
    shape = jax.ShapeDtypeStruct
    dma = pltpu.SemaphoreType.DMA
    results = [
        shape((C, H), F32), shape((E, H), F32), shape((3 * H, H), F32), shape((H, H), F32),
        shape((1, H), F32), shape((2 * H, H), F32), shape((H, H), F32), shape((1, H), F32),
    ]
    args = [
        node_feat[0], send_rows, edge_feat[0], senders, receivers, edge_w1, edge_w2, edge_count,
        edge_gain.reshape(1, H), node_gain.reshape(1, H), node_w1, node_w2, cot_node[0], cot_edge[0],
    ]
    args = [a if a is edge_count else pltpu.with_memory_space_constraint(a, pltpu.HBM) for a in args]
    landing = [pltpu.VMEM(a.shape, a.dtype) for a in args]
    landing[7] = pltpu.SMEM((1, 1), jnp.int32)
    outs = pl.pallas_call(
        functools.partial(kernel, (peers, dps, plane, factor)),
        out_shape=results,
        in_specs=[hbm] * 14,
        out_specs=[vmem] * 8,
        scratch_shapes=landing + [
            dma((14,)),
            pltpu.VMEM((T + C, E), BF16), pltpu.VMEM((H, T), BF16), pltpu.VMEM((H, E), BF16),
            pltpu.VMEM((H, E), F32), pltpu.VMEM((H, E), BF16), pltpu.VMEM((H, E), F32), pltpu.VMEM((H, E), F32),
            pltpu.VMEM((1, E), F32), pltpu.VMEM((H, E), BF16), pltpu.VMEM((H, E), F32),
            pltpu.VMEM((3, GQ, H), BF16), pltpu.VMEM((3, GQ, H), BF16),
            pltpu.VMEM((3, GQ, H), BF16), pltpu.VMEM((3, GQ, H), BF16),
            dma((3,)), dma((3,)), dma((3,)), dma((3,)),
            pltpu.VMEM((4 * H, H), BF16), pltpu.VMEM((group, share, H), BF16),
            pltpu.VMEM((4 * H, H), BF16), pltpu.VMEM((group, share, H), BF16),
            pltpu.VMEM((16, H), BF16), pltpu.VMEM((group, 16, H), BF16),
            pltpu.VMEM((depth, 2 * share, H), BF16), pltpu.VMEM((group, 2 * share, H), BF16),
            dma((5,)), dma((5,)),
        ],
        compiler_params=pltpu.CompilerParams(
            collective_id=0, has_side_effects=True, vmem_limit_bytes=40 * 1024 * 1024
        ),
    )(*args)
    outs = [pltpu.with_memory_space_constraint(a, pltpu.VMEM) for a in outs]
    outs = pl.pallas_call(
        deliver,
        out_shape=results,
        in_specs=[vmem] * 8,
        out_specs=[hbm] * 8,
        scratch_shapes=[dma((8,))],
    )(*outs)
    return (
        outs[0][None], outs[1][None], outs[2], outs[3], outs[4].reshape(H), outs[5], outs[6], outs[7].reshape(H)
    )


def solution(mesh):
    cells = P("dp", "morton", None)
    flat = P("dp", "morton")
    plane = min(16, mesh.shape["morton"] // 2)
    return jax.shard_map(
        functools.partial(on_device, plane),
        mesh=mesh,
        in_specs=(cells, cells, cells, cells, flat, flat, flat, flat, P(), P(), P(), P(), P(), P()),
        out_specs=(cells, cells, P(), P(), P(), P(), P(), P()),
        check_vma=False,
    )
```

```python
import functools

import jax
import jax.numpy as jnp
from jax import lax
from jax.experimental import pallas as pl
from jax.experimental.pallas import tpu as pltpu
from jax.sharding import PartitionSpec as P

MESH = pl.DeviceIdType.MESH
F32 = jnp.float32
BF16 = jnp.bfloat16
GAIN_ROWS = 16


def nn(a, b):
    return lax.dot_general(a, b, (((1,), (0,)), ((), ())), preferred_element_type=F32)


def nt(a, b):
    return lax.dot_general(a, b, (((1,), (1,)), ((), ())), preferred_element_type=F32)


def one_hot(row, depth):
    spot = lax.broadcasted_iota(jnp.int32, (depth, row.shape[1]), 0)
    return jnp.where(spot == row, 1.0, 0.0).astype(BF16)


def sigmoid(a):
    return 0.5 * jnp.tanh(0.5 * a) + 0.5


def silu_parts(a):
    s = sigmoid(a)
    return a * s, s * (1.0 + a * (1.0 - s))


def column_of(row):
    return jnp.broadcast_to(row, (row.shape[1], row.shape[1])).T


def across(column, width):
    return jnp.concatenate([column] * (width // column.shape[1]), axis=1)


def folded(values):
    step = values.shape[0]
    return sum(values[:, i : i + step] for i in range(0, values.shape[1], step))


def row_of(partial):
    return jnp.sum(partial.T, axis=0, keepdims=True)


def normed(b):
    center = b - jnp.mean(b, axis=0, keepdims=True)
    spread = jnp.mean(center * center, axis=0, keepdims=True)
    rs = lax.rsqrt(spread + 1e-05)
    return center * rs, rs


def normed_back(dn, nh, rs):
    m1 = jnp.mean(dn, axis=0, keepdims=True)
    m2 = jnp.mean(dn * nh, axis=0, keepdims=True)
    return rs * (dn - m1 - nh * m2)


def kernel(
    sizes,
    node_hbm, rows_hbm, edge_hbm, snd_hbm, rcv_hbm, w1_hbm, w2_hbm, cnt_hbm,
    eg_hbm, ng_hbm, n1_hbm, n2_hbm, cotn_hbm, cote_hbm,
    gnode, gedge, gw1, gw2, geg, gn1, gn2, gng,
    h_v, rows, e_v, snd, rcv, w1, w2, cnt, eg, ng, n1, n2, cn_v, ce_v, in_sem,
    hot, tab, dsil, nhat, gT,
    gs_send, gs_recv, gb_send, gb_recv, gsem_s, gsem_r, bsem_s, bsem_r,
    a_send, a_recv, a_lift, a_all, b_send, b_recv, b_lift, b_all, psem_s, psem_r,
):
    peers, dps, plane, factor = sizes
    group = plane * dps
    depth = peers // plane
    C, H = h_v.shape
    E = e_v.shape[0]
    GH = rows.shape[1]
    GQ = GH // 4
    T = C + GH
    share = b_recv.shape[1]
    half = peers // 2
    last = group - 1

    m = lax.axis_index("morton")
    core = lax.axis_index("dp")
    level = m // plane
    mine = (m % plane) * dps + core
    low = m < half
    partner = lax.rem(m + half, peers)
    right = lax.rem(m + 1, peers)
    left = lax.rem(m + peers - 1, peers)

    def member(i):
        return (level * plane + i // dps, i % dps)

    def above(z):
        return (z * plane + m % plane, core)

    sources = (
        node_hbm, rows_hbm, edge_hbm, snd_hbm, rcv_hbm, w1_hbm, w2_hbm, cnt_hbm,
        eg_hbm, ng_hbm, n1_hbm, n2_hbm, cotn_hbm, cote_hbm,
    )
    places = (h_v, rows, e_v, snd, rcv, w1, w2, cnt, eg, ng, n1, n2, cn_v, ce_v)
    loads = [
        pltpu.make_async_copy(src, dst, in_sem.at[i]) for i, (src, dst) in enumerate(zip(sources, places))
    ]
    for load in loads:
        load.start()

    barrier = pltpu.get_barrier_semaphore()

    def greet(r, _):
        pl.semaphore_signal(barrier, inc=1, device_id=member(lax.rem(mine + r, group)), device_id_type=MESH)
        return 0

    lax.fori_loop(1, group, greet, 0)

    def greet_above(r, _):
        pl.semaphore_signal(barrier, inc=1, device_id=above(lax.rem(level + r, depth)), device_id_type=MESH)
        return 0

    lax.fori_loop(1, depth, greet_above, 0)
    for side in (left, right):
        pl.semaphore_signal(barrier, inc=1, device_id=(side, core), device_id_type=MESH)

    eye_r = lax.broadcasted_iota(jnp.int32, (H, H), 0)
    eye_c = lax.broadcasted_iota(jnp.int32, (H, H), 1)
    eye = jnp.where(eye_r == eye_c, 1.0, 0.0).astype(BF16)

    lane = lax.broadcasted_iota(jnp.int32, (1, GH), 1)
    first_used = jnp.logical_and(lane < GQ, jnp.logical_not(low))
    last_used = jnp.logical_and(lane >= 3 * GQ, low)
    middle = jnp.logical_and(lane >= GQ, lane < 3 * GQ)
    used = jnp.logical_or(middle, jnp.logical_or(first_used, last_used))
    loads[0].wait()
    loads[1].wait()
    hot_out = one_hot(jnp.where(used, rows[...], -1), C)

    hT = nt(eye, h_v[...]).astype(BF16)
    tab[:, 0:C] = hT
    picked = nn(hT, hot_out).T
    gs_send[0] = (picked[0:GQ] + picked[3 * GQ : 4 * GQ]).astype(BF16)
    gs_send[1] = picked[GQ : 2 * GQ].astype(BF16)
    gs_send[2] = picked[2 * GQ : 3 * GQ].astype(BF16)

    pl.semaphore_wait(barrier, (group - 1) + (depth - 1) + 2)

    ghost_out = [
        pltpu.make_async_remote_copy(
            src_ref=gs_send.at[k], dst_ref=gs_recv.at[k], send_sem=gsem_s.at[k], recv_sem=gsem_r.at[k],
            device_id=(to, core), device_id_type=MESH,
        )
        for k, to in enumerate((partner, left, right))
    ]
    for copy in ghost_out:
        copy.start()

    for load in loads[2:7]:
        load.wait()
    w1T = nt(eye, w1[...].astype(BF16)).astype(BF16)
    w2T = nt(eye, w2[...].astype(BF16)).astype(BF16)
    w1s_T = w1T[:, H : 2 * H]

    hot_s = one_hot(snd[...], T)
    hot_r = one_hot(rcv[...], C)
    hot[0:T] = hot_s
    hot[T : T + C] = hot_r
    eT = nt(eye, e_v[...]).astype(BF16)
    xs = nn(hT, hot_s[0:C]).astype(BF16)
    xr = nn(hT, hot_r).astype(BF16)
    a0 = nn(w1T, jnp.concatenate([eT, xs, xr], axis=0))

    for load in loads[7:12]:
        load.wait()
    gain_e = column_of(eg[...])
    gain_n = column_of(ng[...])
    gain_tile = across(gain_e, E)
    count = cnt[0, 0]

    for copy in ghost_out:
        copy.wait_recv()
    ghosts = jnp.concatenate([gs_recv[0], gs_recv[1], gs_recv[2], gs_recv[0]], axis=0)
    first_here = jnp.logical_and(lane < GQ, low)
    last_here = jnp.logical_and(lane >= 3 * GQ, jnp.logical_not(low))
    here = jnp.logical_or(middle, jnp.logical_or(first_here, last_here))
    ghost_T = jnp.where(here, nt(eye, ghosts), 0.0).astype(BF16)
    tab[:, C:T] = ghost_T

    slot = lax.broadcasted_iota(jnp.int32, (1, E), 1)
    live = jnp.where(slot < count, 1.0, 0.0)

    xg = nn(ghost_T, hot[C:T]).astype(BF16)
    p, d = silu_parts(a0 + nn(w1s_T, xg))
    pT = p.astype(BF16)
    dsil[...] = d
    nh, e_rs = normed(nn(w2T, pT))
    nhat[...] = nh
    msg = (live * (eT.astype(F32) + live * (nh * gain_tile))).astype(BF16)
    agg = nt(msg, hot[T : T + C]).astype(BF16)

    n1b = n1[...].astype(BF16)
    n2b = n2[...].astype(BF16)
    n1T = nt(eye, n1b).astype(BF16)
    n2T = nt(eye, n2b).astype(BF16)
    loads[12].wait()
    yT = jnp.concatenate([hT, agg], axis=0)
    r, dr_ = silu_parts(nn(n1T, yT))
    r = r.astype(BF16)
    nh, rs = normed(nn(n2T, r))
    cnT = nt(eye, cn_v[...])
    acc = folded(cnT * nh)
    ds = normed_back(cnT * across(gain_n, C), nh, rs).astype(BF16)
    dc = (nn(n2b, ds).astype(BF16).astype(F32) * dr_).astype(BF16)
    dyT = nn(n1b, dc).astype(BF16)
    dagg = dyT[H:]
    b_send[0 : 2 * H] = nt(yT, dc).astype(BF16)
    b_send[2 * H : 3 * H] = nt(r, ds).astype(BF16)
    b_send[3 * H :] = jnp.zeros((b_send.shape[0] - 3 * H, H), BF16)
    gain_n_row = row_of(acc)
    node_T = cnT + dyT[0:H].astype(F32)

    def shard(i):
        return pl.ds(pl.multiple_of(i * share, share), share)

    def push(src, dst, phase, to):
        pltpu.make_async_remote_copy(
            src_ref=src, dst_ref=dst, send_sem=psem_s.at[phase], recv_sem=psem_r.at[phase],
            device_id=to, device_id_type=MESH,
        ).start()

    def await_bytes(ref, sem):
        pltpu.make_async_copy(ref, ref, sem).wait()

    def each_member(act):
        def go(r, _):
            act(lax.rem(mine + r, group))
            return 0

        lax.fori_loop(1, group, go, 0)

    def each_level(act):
        def go(r, _):
            act(lax.rem(level + r, depth))
            return 0

        lax.fori_loop(1, depth, go, 0)

    b_others = b_recv.at[pl.ds(0, group - 1)]
    b_levels = b_lift.at[pl.ds(0, depth - 1)]
    b_shares = b_all.at[pl.ds(0, group - 1)]

    each_member(lambda i: push(b_send.at[shard(i)], b_recv.at[mine], 0, member(i)))
    b_recv[mine] = b_send[shard(mine)]

    loads[13].wait()
    w2b = w2[...].astype(BF16)
    g = nt(eye, ce_v[...]) + live * nn(dagg, hot[T : T + C])
    gT[...] = g
    dd = live * g
    nh = nhat[...]
    acc = folded(dd * nh)
    db = normed_back(dd * gain_tile, nh, e_rs).astype(BF16)
    dp = nn(w2b, db).astype(BF16).astype(F32)
    da = (dp * dsil[...]).astype(BF16)

    await_bytes(b_others, psem_r.at[0])
    b_lift[level] = jnp.sum(b_recv[...].astype(F32), axis=0).astype(BF16)
    each_level(lambda z: push(b_lift.at[level], b_lift.at[level], 1, above(z)))

    s_all = nt(hot[...], da).astype(BF16)
    a_send[0:H] = nt(eT, da).astype(BF16)
    a_send[H : 2 * H] = nn(tab[...], s_all[0:T]).astype(BF16)
    a_send[2 * H : 3 * H] = nn(hT, s_all[T:]).astype(BF16)
    a_send[3 * H : 4 * H] = nt(pT, db).astype(BF16)
    a_send[4 * H :] = jnp.zeros((GAIN_ROWS, H), BF16)
    a_send[4 * H : 4 * H + 1] = row_of(acc).astype(BF16)
    a_send[4 * H + 1 : 4 * H + 2] = gain_n_row.astype(BF16)

    wide = share + GAIN_ROWS
    wide_rows = pl.ds(last * share, wide)
    narrow = pl.ds(0, share)
    is_last = mine == last

    def push_edge(i):
        @pl.when(i == last)
        def _():
            push(a_send.at[wide_rows], a_recv.at[mine], 2, member(i))

        @pl.when(i != last)
        def _():
            push(a_send.at[shard(i)], a_recv.at[mine, narrow], 2, member(i))

    each_member(push_edge)

    @pl.when(is_last)
    def _():
        a_recv[mine] = a_send[wide_rows]

    @pl.when(jnp.logical_not(is_last))
    def _():
        a_recv[mine, 0:share] = a_send[shard(mine)]

    w1b = w1[...].astype(BF16)
    dghost = nt(s_all[C:T], w1b[H : 2 * H])
    gb_send[0] = (dghost[0:GQ] + dghost[3 * GQ : 4 * GQ]).astype(BF16)
    gb_send[1] = dghost[GQ : 2 * GQ].astype(BF16)
    gb_send[2] = dghost[2 * GQ : 3 * GQ].astype(BF16)
    ghost_back = [
        pltpu.make_async_remote_copy(
            src_ref=gb_send.at[k], dst_ref=gb_recv.at[k], send_sem=bsem_s.at[k], recv_sem=bsem_r.at[k],
            device_id=(to, core), device_id_type=MESH,
        )
        for k, to in enumerate((partner, right, left))
    ]
    for copy in ghost_back:
        copy.start()

    await_bytes(b_levels, psem_r.at[1])
    b_all[mine] = (jnp.sum(b_lift[...].astype(F32), axis=0) * factor).astype(BF16)
    each_member(lambda i: push(b_all.at[mine], b_all.at[mine], 3, member(i)))

    dx = nn(w1b[0:H], da).astype(BF16).astype(F32)
    half_e = E // 2
    gedge[0:half_e] = (gT[:, 0:half_e] + dx[:, 0:half_e]).T

    @pl.when(is_last)
    def _():
        await_bytes(a_recv.at[pl.ds(0, group - 1)], psem_r.at[2])
        a_lift[level] = jnp.sum(a_recv[...].astype(F32), axis=0).astype(BF16)
        each_level(lambda z: push(a_lift.at[level], a_lift.at[level], 4, above(z)))

    @pl.when(jnp.logical_not(is_last))
    def _():
        await_bytes(a_recv.at[pl.ds(0, group - 1), narrow], psem_r.at[2])
        a_lift[level, 0:share] = jnp.sum(a_recv[:, 0:share].astype(F32), axis=0).astype(BF16)
        each_level(lambda z: push(a_lift.at[level, narrow], a_lift.at[level, narrow], 4, above(z)))

    gedge[half_e:E] = (gT[:, half_e:E] + dx[:, half_e:E]).T
    own = nt(s_all[0:C], w1b[H : 2 * H]).astype(BF16).astype(F32)
    own = own + nt(s_all[T:], w1b[2 * H : 3 * H]).astype(BF16).astype(F32)
    gnode[...] = node_T.T + own

    @pl.when(is_last)
    def _():
        await_bytes(a_lift.at[pl.ds(0, depth - 1)], psem_r.at[4])
        total = (jnp.sum(a_lift[...].astype(F32), axis=0) * factor).astype(BF16)
        a_all[wide_rows] = total
        each_member(lambda i: push(a_all.at[wide_rows], a_all.at[wide_rows], 5, member(i)))

    @pl.when(jnp.logical_not(is_last))
    def _():
        await_bytes(a_lift.at[pl.ds(0, depth - 1), narrow], psem_r.at[4])
        total = (jnp.sum(a_lift[:, 0:share].astype(F32), axis=0) * factor).astype(BF16)
        a_all[shard(mine)] = total
        each_member(lambda i: push(a_all.at[shard(mine)], a_all.at[shard(mine)], 5, member(i)))

    for copy in ghost_back:
        copy.wait_recv()
    back = jnp.concatenate([gb_recv[0], gb_recv[1], gb_recv[2], gb_recv[0]], axis=0)
    gnode[...] += nn(hot_out, back)

    await_bytes(b_shares, psem_r.at[3])
    gn1[...] = b_all[0 : 2 * H // share].astype(F32).reshape(2 * H, H)
    gn2[...] = b_all[2 * H // share : 3 * H // share].astype(F32).reshape(H, H)

    for copy in ghost_out + ghost_back:
        copy.wait_send()
    await_bytes(b_others, psem_s.at[0])
    await_bytes(b_levels, psem_s.at[1])
    await_bytes(b_shares, psem_s.at[3])

    without_share = a_all.at[pl.ds(0, (group - 1) * share)]
    without_gains = a_all.at[pl.ds(0, (group - 1) * share + GAIN_ROWS)]

    @pl.when(is_last)
    def _():
        await_bytes(without_share, psem_s.at[2])
        await_bytes(a_lift.at[pl.ds(0, depth - 1)], psem_s.at[4])
        await_bytes(a_recv.at[pl.ds(0, group - 1)], psem_s.at[5])
        await_bytes(without_share, psem_r.at[5])

    @pl.when(jnp.logical_not(is_last))
    def _():
        await_bytes(without_gains, psem_s.at[2])
        await_bytes(a_lift.at[pl.ds(0, depth - 1), narrow], psem_s.at[4])
        await_bytes(a_recv.at[pl.ds(0, group - 1), narrow], psem_s.at[5])
        await_bytes(without_gains, psem_r.at[5])

    gw1[...] = a_all[0 : 3 * H].astype(F32)
    gw2[...] = a_all[3 * H : 4 * H].astype(F32)
    tail = a_all[4 * H : 4 * H + GAIN_ROWS].astype(F32)
    geg[...] = tail[0:1]
    gng[...] = tail[1:2]


def deliver(*refs):
    n = len(refs) // 2
    sem = refs[-1]
    copies = [pltpu.make_async_copy(refs[i], refs[n + i], sem.at[i]) for i in range(n)]
    for copy in copies:
        copy.start()
    for copy in copies:
        copy.wait()


def on_device(
    plane, node_feat, edge_feat, cot_node, cot_edge, senders, receivers, send_rows, edge_count,
    edge_w1, edge_w2, edge_gain, node_w1, node_w2, node_gain,
):
    peers, dps = lax.axis_size("morton"), lax.axis_size("dp")
    C, H = node_feat.shape[1:]
    E = edge_feat.shape[1]
    GH = send_rows.shape[1]
    GQ = GH // 4
    T = C + GH
    group = plane * dps
    depth = peers // plane
    share = 4 * H // group
    factor = (dps * peers * E) ** -0.5
    vmem = pl.BlockSpec(memory_space=pltpu.VMEM)
    hbm = pl.BlockSpec(memory_space=pltpu.HBM)
    shape = jax.ShapeDtypeStruct
    dma = pltpu.SemaphoreType.DMA
    results = [
        shape((C, H), F32), shape((E, H), F32), shape((3 * H, H), F32), shape((H, H), F32),
        shape((1, H), F32), shape((2 * H, H), F32), shape((H, H), F32), shape((1, H), F32),
    ]
    args = [
        node_feat[0], send_rows, edge_feat[0], senders, receivers, edge_w1, edge_w2, edge_count,
        edge_gain.reshape(1, H), node_gain.reshape(1, H), node_w1, node_w2, cot_node[0], cot_edge[0],
    ]
    args = [a if a is edge_count else pltpu.with_memory_space_constraint(a, pltpu.HBM) for a in args]
    landing = [pltpu.VMEM(a.shape, a.dtype) for a in args]
    landing[7] = pltpu.SMEM((1, 1), jnp.int32)
    outs = pl.pallas_call(
        functools.partial(kernel, (peers, dps, plane, factor)),
        out_shape=results,
        in_specs=[hbm] * 14,
        out_specs=[vmem] * 8,
        scratch_shapes=landing + [
            dma((14,)),
            pltpu.VMEM((T + C, E), BF16), pltpu.VMEM((H, T), BF16),
            pltpu.VMEM((H, E), F32), pltpu.VMEM((H, E), F32), pltpu.VMEM((H, E), F32),
            pltpu.VMEM((3, GQ, H), BF16), pltpu.VMEM((3, GQ, H), BF16),
            pltpu.VMEM((3, GQ, H), BF16), pltpu.VMEM((3, GQ, H), BF16),
            dma((3,)), dma((3,)), dma((3,)), dma((3,)),
            pltpu.VMEM((4 * H + GAIN_ROWS, H), BF16), pltpu.VMEM((group, share + GAIN_ROWS, H), BF16),
            pltpu.VMEM((depth, share + GAIN_ROWS, H), BF16), pltpu.VMEM((4 * H + GAIN_ROWS, H), BF16),
            pltpu.VMEM((4 * H, H), BF16), pltpu.VMEM((group, share, H), BF16),
            pltpu.VMEM((depth, share, H), BF16), pltpu.VMEM((group, share, H), BF16),
            dma((6,)), dma((6,)),
        ],
        compiler_params=pltpu.CompilerParams(
            collective_id=0, has_side_effects=True, vmem_limit_bytes=40 * 1024 * 1024
        ),
    )(*args)
    outs = [pltpu.with_memory_space_constraint(a, pltpu.VMEM) for a in outs]
    outs = pl.pallas_call(
        deliver,
        out_shape=results,
        in_specs=[vmem] * 8,
        out_specs=[hbm] * 8,
        scratch_shapes=[dma((8,))],
    )(*outs)
    return (
        outs[0][None], outs[1][None], outs[2], outs[3], outs[4].reshape(H), outs[5], outs[6], outs[7].reshape(H)
    )


def solution(mesh):
    cells = P("dp", "morton", None)
    flat = P("dp", "morton")
    plane = min(16, mesh.shape["morton"] // 2)
    return jax.shard_map(
        functools.partial(on_device, plane),
        mesh=mesh,
        in_specs=(cells, cells, cells, cells, flat, flat, flat, flat, P(), P(), P(), P(), P(), P()),
        out_specs=(cells, cells, P(), P(), P(), P(), P(), P()),
        check_vma=False,
    )
```

```python
import functools

import jax
import jax.numpy as jnp
from jax import lax
from jax.experimental import pallas as pl
from jax.experimental.pallas import tpu as pltpu
from jax.sharding import PartitionSpec as P

MESH = pl.DeviceIdType.MESH
F32 = jnp.float32
BF16 = jnp.bfloat16
GAIN_ROWS = 16


def nn(a, b):
    return lax.dot_general(a, b, (((1,), (0,)), ((), ())), preferred_element_type=F32)


def nt(a, b):
    return lax.dot_general(a, b, (((1,), (1,)), ((), ())), preferred_element_type=F32)


def one_hot(row, depth):
    spot = lax.broadcasted_iota(jnp.int32, (depth, row.shape[1]), 0)
    return jnp.where(spot == row, 1.0, 0.0).astype(BF16)


def sigmoid(a):
    return 0.5 * jnp.tanh(0.5 * a) + 0.5


def silu_parts(a):
    s = sigmoid(a)
    return a * s, s * (1.0 + a * (1.0 - s))


def column_of(row):
    return jnp.broadcast_to(row, (row.shape[1], row.shape[1])).T


def across(column, width):
    return jnp.concatenate([column] * (width // column.shape[1]), axis=1)


def folded(values):
    step = values.shape[0]
    return sum(values[:, i : i + step] for i in range(0, values.shape[1], step))


def row_of(partial):
    return jnp.sum(partial.T, axis=0, keepdims=True)


def normed(b):
    center = b - jnp.mean(b, axis=0, keepdims=True)
    spread = jnp.mean(center * center, axis=0, keepdims=True)
    rs = lax.rsqrt(spread + 1e-05)
    return center * rs, rs


def normed_back(dn, nh, rs):
    m1 = jnp.mean(dn, axis=0, keepdims=True)
    m2 = jnp.mean(dn * nh, axis=0, keepdims=True)
    return rs * (dn - m1 - nh * m2)


def kernel(
    sizes,
    node_hbm, rows_hbm, edge_hbm, snd_hbm, rcv_hbm, w1_hbm, w2_hbm, cnt_hbm,
    eg_hbm, ng_hbm, n1_hbm, n2_hbm, cotn_hbm, cote_hbm,
    gnode, gedge, gw1, gw2, geg, gn1, gn2, gng,
    h_v, rows, e_v, snd, rcv, w1, w2, cnt, eg, ng, n1, n2, cn_v, ce_v, in_sem,
    hot, xT, ceT, dsil, nhat, gT,
    gs_send, gs_recv, gb_send, gb_recv, gsem_s, gsem_r, bsem_s, bsem_r,
    a_send, a_recv, a_lift, a_all, b_send, b_recv, b_lift, b_all, psem_s, psem_r,
):
    peers, dps, plane, factor = sizes
    group = plane * dps
    depth = peers // plane
    C, H = h_v.shape
    E = e_v.shape[0]
    GH = rows.shape[1]
    GQ = GH // 4
    T = C + GH
    share = b_recv.shape[1]
    half = peers // 2
    last = group - 1

    m = lax.axis_index("morton")
    core = lax.axis_index("dp")
    level = m // plane
    mine = (m % plane) * dps + core
    low = m < half
    partner = lax.rem(m + half, peers)
    right = lax.rem(m + 1, peers)
    left = lax.rem(m + peers - 1, peers)

    def member(i):
        return (level * plane + i // dps, i % dps)

    def above(z):
        return (z * plane + m % plane, core)

    barrier = pltpu.get_barrier_semaphore()

    def greet(to):
        pl.semaphore_signal(barrier, inc=1, device_id=to, device_id_type=MESH)

    def each_member(act):
        def go(r, _):
            act(lax.rem(mine + r, group))
            return 0

        lax.fori_loop(1, group, go, 0)

    def each_level(act):
        def go(r, _):
            act(lax.rem(level + r, depth))
            return 0

        lax.fori_loop(1, depth, go, 0)

    greet((partner, core))
    greet((left, core))
    greet((right, core))
    sources = (
        node_hbm, rows_hbm, edge_hbm, snd_hbm, rcv_hbm, w1_hbm, w2_hbm, cnt_hbm,
        eg_hbm, ng_hbm, n1_hbm, n2_hbm, cotn_hbm, cote_hbm,
    )
    places = (h_v, rows, e_v, snd, rcv, w1, w2, cnt, eg, ng, n1, n2, cn_v, ce_v)
    loads = [
        pltpu.make_async_copy(src, dst, in_sem.at[i]) for i, (src, dst) in enumerate(zip(sources, places))
    ]
    for load in loads:
        load.start()

    each_level(lambda z: greet(above(z)))
    each_member(lambda i: greet(member(i)))

    eye_r = lax.broadcasted_iota(jnp.int32, (H, H), 0)
    eye_c = lax.broadcasted_iota(jnp.int32, (H, H), 1)
    eye = jnp.where(eye_r == eye_c, 1.0, 0.0).astype(BF16)

    lane = lax.broadcasted_iota(jnp.int32, (1, GH), 1)
    first_used = jnp.logical_and(lane < GQ, jnp.logical_not(low))
    last_used = jnp.logical_and(lane >= 3 * GQ, low)
    middle = jnp.logical_and(lane >= GQ, lane < 3 * GQ)
    used = jnp.logical_or(middle, jnp.logical_or(first_used, last_used))
    loads[0].wait()
    loads[1].wait()
    hot_out = one_hot(jnp.where(used, rows[...], -1), C)

    hT = nt(eye, h_v[...]).astype(BF16)
    picked = nn(hT, hot_out).T
    gs_send[0] = (picked[0:GQ] + picked[3 * GQ : 4 * GQ]).astype(BF16)
    gs_send[1] = picked[GQ : 2 * GQ].astype(BF16)
    gs_send[2] = picked[2 * GQ : 3 * GQ].astype(BF16)

    pl.semaphore_wait(barrier, (group - 1) + (depth - 1) + 3)

    ghost_out = [
        pltpu.make_async_remote_copy(
            src_ref=gs_send.at[k], dst_ref=gs_recv.at[k], send_sem=gsem_s.at[k], recv_sem=gsem_r.at[k],
            device_id=(to, core), device_id_type=MESH,
        )
        for k, to in enumerate((partner, left, right))
    ]
    for copy in ghost_out:
        copy.start()

    for load in loads[2:7]:
        load.wait()
    w1T = nt(eye, w1[...].astype(BF16)).astype(BF16)
    w2T = nt(eye, w2[...].astype(BF16)).astype(BF16)
    w1s_T = w1T[:, H : 2 * H]

    hot_s = one_hot(snd[...], T)
    hot_r = one_hot(rcv[...], C)
    hot[0:T] = hot_s
    hot[T : T + C] = hot_r
    eT = nt(eye, e_v[...]).astype(BF16)
    xs = nn(hT, hot_s[0:C]).astype(BF16)
    xr = nn(hT, hot_r).astype(BF16)
    a0 = nn(w1T, jnp.concatenate([eT, xs, xr], axis=0))
    xT[0:H] = eT
    xT[H : 2 * H] = xs
    xT[2 * H : 3 * H] = xr

    for load in loads[7:]:
        load.wait()
    ceT[...] = nt(eye, ce_v[...]).astype(BF16)
    cnT = nt(eye, cn_v[...])
    n1b = n1[...].astype(BF16)
    n2b = n2[...].astype(BF16)
    n1T = nt(eye, n1b).astype(BF16)
    n2T = nt(eye, n2b).astype(BF16)
    w1b = w1[...].astype(BF16)
    w2b = w2[...].astype(BF16)
    slot = lax.broadcasted_iota(jnp.int32, (1, E), 1)
    gain_e = column_of(eg[...])
    gain_n = column_of(ng[...])
    gain_tile = across(gain_e, E)
    count = cnt[0, 0]

    for copy in ghost_out:
        copy.wait_recv()
    ghosts = jnp.concatenate([gs_recv[0], gs_recv[1], gs_recv[2], gs_recv[0]], axis=0)
    first_here = jnp.logical_and(lane < GQ, low)
    last_here = jnp.logical_and(lane >= 3 * GQ, jnp.logical_not(low))
    here = jnp.logical_or(middle, jnp.logical_or(first_here, last_here))
    ghost_T = jnp.where(here, nt(eye, ghosts), 0.0).astype(BF16)

    live = jnp.where(slot < count, 1.0, 0.0)

    xg = nn(ghost_T, hot[C:T]).astype(BF16)
    p, d = silu_parts(a0 + nn(w1s_T, xg))
    xT[H : 2 * H] += xg
    pT = p.astype(BF16)
    dsil[...] = d
    nh, e_rs = normed(nn(w2T, pT))
    nhat[...] = nh
    msg = (live * (eT.astype(F32) + live * (nh * gain_tile))).astype(BF16)
    agg = nt(msg, hot[T : T + C]).astype(BF16)

    yT = jnp.concatenate([hT, agg], axis=0)
    r, dr_ = silu_parts(nn(n1T, yT))
    r = r.astype(BF16)
    nh, rs = normed(nn(n2T, r))
    acc = folded(cnT * nh)
    ds = normed_back(cnT * across(gain_n, C), nh, rs).astype(BF16)
    dc = (nn(n2b, ds).astype(BF16).astype(F32) * dr_).astype(BF16)
    dyT = nn(n1b, dc).astype(BF16)
    dagg = dyT[H:]
    b_send[0 : 2 * H] = nt(yT, dc).astype(BF16)
    b_send[2 * H : 3 * H] = nt(r, ds).astype(BF16)
    b_send[3 * H :] = jnp.zeros((b_send.shape[0] - 3 * H, H), BF16)
    gain_n_row = row_of(acc)
    node_T = cnT + dyT[0:H].astype(F32)

    def shard(i):
        return pl.ds(pl.multiple_of(i * share, share), share)

    def push(src, dst, phase, to):
        pltpu.make_async_remote_copy(
            src_ref=src, dst_ref=dst, send_sem=psem_s.at[phase], recv_sem=psem_r.at[phase],
            device_id=to, device_id_type=MESH,
        ).start()

    def await_bytes(ref, sem):
        pltpu.make_async_copy(ref, ref, sem).wait()

    b_others = b_recv.at[pl.ds(0, group - 1)]
    b_levels = b_lift.at[pl.ds(0, depth - 1)]
    b_shares = b_all.at[pl.ds(0, group - 1)]

    each_member(lambda i: push(b_send.at[shard(i)], b_recv.at[mine], 0, member(i)))
    b_recv[mine] = b_send[shard(mine)]

    g = ceT[...].astype(F32) + live * nn(dagg, hot[T : T + C])
    gT[...] = g
    dd = live * g
    nh = nhat[...]
    acc = folded(dd * nh)
    db = normed_back(dd * gain_tile, nh, e_rs).astype(BF16)
    dp = nn(w2b, db).astype(BF16).astype(F32)
    da = (dp * dsil[...]).astype(BF16)

    a_send[0 : 3 * H] = nt(xT[...], da).astype(BF16)
    a_send[3 * H : 4 * H] = nt(pT, db).astype(BF16)
    gain_row = lax.broadcasted_iota(jnp.int32, (GAIN_ROWS, H), 0)
    gains = jnp.where(gain_row == 0, row_of(acc), jnp.where(gain_row == 1, gain_n_row, 0.0))
    a_send[4 * H :] = gains.astype(BF16)

    wide = share + GAIN_ROWS
    wide_rows = pl.ds(last * share, wide)
    narrow = pl.ds(0, share)
    is_last = mine == last

    def push_edge(i):
        @pl.when(i == last)
        def _():
            push(a_send.at[wide_rows], a_recv.at[mine], 2, member(i))

        @pl.when(i != last)
        def _():
            push(a_send.at[shard(i)], a_recv.at[mine, narrow], 2, member(i))

    each_member(push_edge)

    @pl.when(is_last)
    def _():
        a_recv[mine] = a_send[wide_rows]

    @pl.when(jnp.logical_not(is_last))
    def _():
        a_recv[mine, 0:share] = a_send[shard(mine)]

    s_all = nt(hot[...], da).astype(BF16)
    dghost = nt(s_all[C:T], w1b[H : 2 * H])
    gb_send[0] = (dghost[0:GQ] + dghost[3 * GQ : 4 * GQ]).astype(BF16)
    gb_send[1] = dghost[GQ : 2 * GQ].astype(BF16)
    gb_send[2] = dghost[2 * GQ : 3 * GQ].astype(BF16)
    ghost_back = [
        pltpu.make_async_remote_copy(
            src_ref=gb_send.at[k], dst_ref=gb_recv.at[k], send_sem=bsem_s.at[k], recv_sem=bsem_r.at[k],
            device_id=(to, core), device_id_type=MESH,
        )
        for k, to in enumerate((partner, right, left))
    ]
    for copy in ghost_back:
        copy.start()

    await_bytes(b_others, psem_r.at[0])
    b_lift[level] = jnp.sum(b_recv[...].astype(F32), axis=0).astype(BF16)
    each_level(lambda z: push(b_lift.at[level], b_lift.at[level], 1, above(z)))

    dx = nn(w1b[0:H], da).astype(BF16).astype(F32)
    half_e = E // 2
    gedge[0:half_e] = (gT[:, 0:half_e] + dx[:, 0:half_e]).T

    @pl.when(is_last)
    def _():
        await_bytes(a_recv.at[pl.ds(0, group - 1)], psem_r.at[2])
        a_lift[level] = jnp.sum(a_recv[...].astype(F32), axis=0).astype(BF16)
        each_level(lambda z: push(a_lift.at[level], a_lift.at[level], 4, above(z)))

    @pl.when(jnp.logical_not(is_last))
    def _():
        await_bytes(a_recv.at[pl.ds(0, group - 1), narrow], psem_r.at[2])
        a_lift[level, 0:share] = jnp.sum(a_recv[:, 0:share].astype(F32), axis=0).astype(BF16)
        each_level(lambda z: push(a_lift.at[level, narrow], a_lift.at[level, narrow], 4, above(z)))

    await_bytes(b_levels, psem_r.at[1])
    b_all[mine] = (jnp.sum(b_lift[...].astype(F32), axis=0) * factor).astype(BF16)
    each_member(lambda i: push(b_all.at[mine], b_all.at[mine], 3, member(i)))

    gedge[half_e:E] = (gT[:, half_e:E] + dx[:, half_e:E]).T
    own = nt(s_all[0:C], w1b[H : 2 * H]).astype(BF16).astype(F32)
    own = own + nt(s_all[T:], w1b[2 * H : 3 * H]).astype(BF16).astype(F32)
    gnode[...] = node_T.T + own

    @pl.when(is_last)
    def _():
        await_bytes(a_lift.at[pl.ds(0, depth - 1)], psem_r.at[4])
        total = (jnp.sum(a_lift[...].astype(F32), axis=0) * factor).astype(BF16)
        a_all[wide_rows] = total
        each_member(lambda i: push(a_all.at[wide_rows], a_all.at[wide_rows], 5, member(i)))

    @pl.when(jnp.logical_not(is_last))
    def _():
        await_bytes(a_lift.at[pl.ds(0, depth - 1), narrow], psem_r.at[4])
        total = (jnp.sum(a_lift[:, 0:share].astype(F32), axis=0) * factor).astype(BF16)
        a_all[shard(mine)] = total
        each_member(lambda i: push(a_all.at[shard(mine)], a_all.at[shard(mine)], 5, member(i)))

    for copy in ghost_back:
        copy.wait_recv()
    back = jnp.concatenate([gb_recv[0], gb_recv[1], gb_recv[2], gb_recv[0]], axis=0)
    gnode[...] += nn(hot_out, back)

    await_bytes(b_shares, psem_r.at[3])
    gn1[...] = b_all[0 : 2 * H // share].astype(F32).reshape(2 * H, H)
    gn2[...] = b_all[2 * H // share : 3 * H // share].astype(F32).reshape(H, H)

    for copy in ghost_out + ghost_back:
        copy.wait_send()
    await_bytes(b_others, psem_s.at[0])
    await_bytes(b_levels, psem_s.at[1])
    await_bytes(b_shares, psem_s.at[3])

    without_share = a_all.at[pl.ds(0, (group - 1) * share)]
    without_gains = a_all.at[pl.ds(0, (group - 1) * share + GAIN_ROWS)]

    @pl.when(is_last)
    def _():
        await_bytes(without_share, psem_s.at[2])
        await_bytes(a_lift.at[pl.ds(0, depth - 1)], psem_s.at[4])
        await_bytes(a_recv.at[pl.ds(0, group - 1)], psem_s.at[5])
        await_bytes(without_share, psem_r.at[5])

    @pl.when(jnp.logical_not(is_last))
    def _():
        await_bytes(without_gains, psem_s.at[2])
        await_bytes(a_lift.at[pl.ds(0, depth - 1), narrow], psem_s.at[4])
        await_bytes(a_recv.at[pl.ds(0, group - 1), narrow], psem_s.at[5])
        await_bytes(without_gains, psem_r.at[5])

    gw1[...] = a_all[0 : 3 * H].astype(F32)
    gw2[...] = a_all[3 * H : 4 * H].astype(F32)
    tail = a_all[4 * H : 4 * H + GAIN_ROWS].astype(F32)
    geg[...] = tail[0:1]
    gng[...] = tail[1:2]


def deliver(*refs):
    n = len(refs) // 2
    sem = refs[-1]
    copies = [pltpu.make_async_copy(refs[i], refs[n + i], sem.at[i]) for i in range(n)]
    for copy in copies:
        copy.start()
    for copy in copies:
        copy.wait()


def on_device(
    plane, node_feat, edge_feat, cot_node, cot_edge, senders, receivers, send_rows, edge_count,
    edge_w1, edge_w2, edge_gain, node_w1, node_w2, node_gain,
):
    peers, dps = lax.axis_size("morton"), lax.axis_size("dp")
    C, H = node_feat.shape[1:]
    E = edge_feat.shape[1]
    GH = send_rows.shape[1]
    GQ = GH // 4
    T = C + GH
    group = plane * dps
    depth = peers // plane
    share = 4 * H // group
    factor = (dps * peers * E) ** -0.5
    vmem = pl.BlockSpec(memory_space=pltpu.VMEM)
    hbm = pl.BlockSpec(memory_space=pltpu.HBM)
    shape = jax.ShapeDtypeStruct
    dma = pltpu.SemaphoreType.DMA
    results = [
        shape((C, H), F32), shape((E, H), F32), shape((3 * H, H), F32), shape((H, H), F32),
        shape((1, H), F32), shape((2 * H, H), F32), shape((H, H), F32), shape((1, H), F32),
    ]
    args = [
        node_feat[0], send_rows, edge_feat[0], senders, receivers, edge_w1, edge_w2, edge_count,
        edge_gain.reshape(1, H), node_gain.reshape(1, H), node_w1, node_w2, cot_node[0], cot_edge[0],
    ]
    args = [a if a is edge_count else pltpu.with_memory_space_constraint(a, pltpu.HBM) for a in args]
    landing = [pltpu.VMEM(a.shape, a.dtype) for a in args]
    landing[7] = pltpu.SMEM((1, 1), jnp.int32)
    outs = pl.pallas_call(
        functools.partial(kernel, (peers, dps, plane, factor)),
        out_shape=results,
        in_specs=[hbm] * 14,
        out_specs=[vmem] * 8,
        scratch_shapes=landing + [
            dma((14,)),
            pltpu.VMEM((T + C, E), BF16), pltpu.VMEM((3 * H, E), BF16), pltpu.VMEM((H, E), BF16),
            pltpu.VMEM((H, E), F32), pltpu.VMEM((H, E), F32), pltpu.VMEM((H, E), F32),
            pltpu.VMEM((3, GQ, H), BF16), pltpu.VMEM((3, GQ, H), BF16),
            pltpu.VMEM((3, GQ, H), BF16), pltpu.VMEM((3, GQ, H), BF16),
            dma((3,)), dma((3,)), dma((3,)), dma((3,)),
            pltpu.VMEM((4 * H + GAIN_ROWS, H), BF16), pltpu.VMEM((group, share + GAIN_ROWS, H), BF16),
            pltpu.VMEM((depth, share + GAIN_ROWS, H), BF16), pltpu.VMEM((4 * H + GAIN_ROWS, H), BF16),
            pltpu.VMEM((4 * H, H), BF16), pltpu.VMEM((group, share, H), BF16),
            pltpu.VMEM((depth, share, H), BF16), pltpu.VMEM((group, share, H), BF16),
            dma((6,)), dma((6,)),
        ],
        compiler_params=pltpu.CompilerParams(
            collective_id=0, has_side_effects=True, vmem_limit_bytes=40 * 1024 * 1024
        ),
    )(*args)
    outs = [pltpu.with_memory_space_constraint(a, pltpu.VMEM) for a in outs]
    outs = pl.pallas_call(
        deliver,
        out_shape=results,
        in_specs=[vmem] * 8,
        out_specs=[hbm] * 8,
        scratch_shapes=[dma((8,))],
    )(*outs)
    return (
        outs[0][None], outs[1][None], outs[2], outs[3], outs[4].reshape(H), outs[5], outs[6], outs[7].reshape(H)
    )


def solution(mesh):
    cells = P("dp", "morton", None)
    flat = P("dp", "morton")
    plane = min(16, mesh.shape["morton"] // 2)
    return jax.shard_map(
        functools.partial(on_device, plane),
        mesh=mesh,
        in_specs=(cells, cells, cells, cells, flat, flat, flat, flat, P(), P(), P(), P(), P(), P()),
        out_specs=(cells, cells, P(), P(), P(), P(), P(), P()),
        check_vma=False,
    )
```

```python
import functools

import jax
import jax.numpy as jnp
from jax import lax
from jax.experimental import pallas as pl
from jax.experimental.pallas import tpu as pltpu
from jax.sharding import PartitionSpec as P

MESH = pl.DeviceIdType.MESH
F32 = jnp.float32
BF16 = jnp.bfloat16
GAIN_ROWS = 16


SIDE = 4
PIECES = 4


def ring(offset, size):
    return min(offset, size - offset)


def farthest_first(plane, dps):
    steps = [(ox, oy, oc) for ox in range(plane // SIDE) for oy in range(SIDE) for oc in range(dps)]
    return sorted(steps[1:], key=lambda o: -(ring(o[0], SIDE) + ring(o[1], SIDE)))


def nn(a, b):
    return lax.dot_general(a, b, (((1,), (0,)), ((), ())), preferred_element_type=F32)


def nt(a, b):
    return lax.dot_general(a, b, (((1,), (1,)), ((), ())), preferred_element_type=F32)


def one_hot(row, depth):
    spot = lax.broadcasted_iota(jnp.int32, (depth, row.shape[1]), 0)
    return jnp.where(spot == row, 1.0, 0.0).astype(BF16)


def sigmoid(a):
    return 0.5 * jnp.tanh(0.5 * a) + 0.5


def silu_parts(a):
    s = sigmoid(a)
    return a * s, s * (1.0 + a * (1.0 - s))


def column_of(row):
    return jnp.broadcast_to(row, (row.shape[1], row.shape[1])).T


def across(column, width):
    return jnp.concatenate([column] * (width // column.shape[1]), axis=1)


def folded(values):
    step = values.shape[0]
    return sum(values[:, i : i + step] for i in range(0, values.shape[1], step))


def row_of(partial):
    return jnp.sum(partial.T, axis=0, keepdims=True)


def normed(b):
    center = b - jnp.mean(b, axis=0, keepdims=True)
    spread = jnp.mean(center * center, axis=0, keepdims=True)
    rs = lax.rsqrt(spread + 1e-05)
    return center * rs, rs


def normed_back(dn, nh, rs):
    m1 = jnp.mean(dn, axis=0, keepdims=True)
    m2 = jnp.mean(dn * nh, axis=0, keepdims=True)
    return rs * (dn - m1 - nh * m2)


def kernel(
    sizes,
    node_hbm, rows_hbm, edge_hbm, snd_hbm, rcv_hbm, w1_hbm, w2_hbm, cnt_hbm,
    eg_hbm, ng_hbm, n1_hbm, n2_hbm, cotn_hbm, cote_hbm,
    gnode, gedge, gw1, gw2, geg, gn1, gn2, gng,
    h_v, rows, e_v, snd, rcv, w1, w2, cnt, eg, ng, n1, n2, cn_v, ce_v, in_sem,
    hot, xT, ceT, dsil, nhat, gT,
    gs_send, gs_recv, gb_send, gb_recv, gsem_s, gsem_r, bsem_s, bsem_r,
    a_send, a_recv, a_lift, a_all, b_send, b_recv, b_lift, b_all, psem_s, psem_r,
):
    peers, dps, plane, factor = sizes
    group = plane * dps
    depth = peers // plane
    C, H = h_v.shape
    E = e_v.shape[0]
    GH = rows.shape[1]
    GQ = GH // 4
    T = C + GH
    share = b_recv.shape[1]
    half = peers // 2
    last = group - 1

    m = lax.axis_index("morton")
    core = lax.axis_index("dp")
    level = m // plane
    mine = (m % plane) * dps + core
    low = m < half
    partner = lax.rem(m + half, peers)
    right = lax.rem(m + 1, peers)
    left = lax.rem(m + peers - 1, peers)

    def member(i):
        return (level * plane + i // dps, i % dps)

    mx = (m % plane) // SIDE
    my = m % SIDE

    def above(z):
        return (z * plane + m % plane, core)

    barrier = pltpu.get_barrier_semaphore()

    def greet(to):
        pl.semaphore_signal(barrier, inc=1, device_id=to, device_id_type=MESH)

    def each_member(act):
        for ox, oy, oc in farthest_first(plane, dps):
            column = lax.rem(mx + ox, SIDE) * SIDE + lax.rem(my + oy, SIDE)
            other = lax.rem(core + oc, dps)
            act(column * dps + other, (level * plane + column, other))

    def each_level(act):
        for o in sorted(range(1, depth), key=lambda o: -ring(o, depth)):
            act(above(lax.rem(level + o, depth)))

    greet((partner, core))
    greet((left, core))
    greet((right, core))
    sources = (
        node_hbm, rows_hbm, edge_hbm, snd_hbm, rcv_hbm, w1_hbm, w2_hbm, cnt_hbm,
        eg_hbm, ng_hbm, n1_hbm, n2_hbm, cotn_hbm, cote_hbm,
    )
    places = (h_v, rows, e_v, snd, rcv, w1, w2, cnt, eg, ng, n1, n2, cn_v, ce_v)
    loads = [
        pltpu.make_async_copy(src, dst, in_sem.at[i]) for i, (src, dst) in enumerate(zip(sources, places))
    ]
    for load in loads:
        load.start()

    each_level(greet)
    each_member(lambda i, to: greet(to))

    eye_r = lax.broadcasted_iota(jnp.int32, (H, H), 0)
    eye_c = lax.broadcasted_iota(jnp.int32, (H, H), 1)
    eye = jnp.where(eye_r == eye_c, 1.0, 0.0).astype(BF16)

    lane = lax.broadcasted_iota(jnp.int32, (1, GH), 1)
    first_used = jnp.logical_and(lane < GQ, jnp.logical_not(low))
    last_used = jnp.logical_and(lane >= 3 * GQ, low)
    middle = jnp.logical_and(lane >= GQ, lane < 3 * GQ)
    used = jnp.logical_or(middle, jnp.logical_or(first_used, last_used))
    loads[0].wait()
    loads[1].wait()
    hot_out = one_hot(jnp.where(used, rows[...], -1), C)

    hT = nt(eye, h_v[...]).astype(BF16)
    picked = nn(hT, hot_out).T
    gs_send[0] = (picked[0:GQ] + picked[3 * GQ : 4 * GQ]).astype(BF16)
    gs_send[1] = picked[GQ : 2 * GQ].astype(BF16)
    gs_send[2] = picked[2 * GQ : 3 * GQ].astype(BF16)

    pl.semaphore_wait(barrier, (group - 1) + (depth - 1) + 3)

    ghost_out = [
        pltpu.make_async_remote_copy(
            src_ref=gs_send.at[k], dst_ref=gs_recv.at[k], send_sem=gsem_s.at[k], recv_sem=gsem_r.at[k],
            device_id=(to, core), device_id_type=MESH,
        )
        for k, to in enumerate((partner, left, right))
    ]
    for copy in ghost_out:
        copy.start()

    for load in loads[2:7]:
        load.wait()
    w1T = nt(eye, w1[...].astype(BF16)).astype(BF16)
    w2T = nt(eye, w2[...].astype(BF16)).astype(BF16)
    w1s_T = w1T[:, H : 2 * H]

    hot_s = one_hot(snd[...], T)
    hot_r = one_hot(rcv[...], C)
    hot[0:T] = hot_s
    hot[T : T + C] = hot_r
    eT = nt(eye, e_v[...]).astype(BF16)
    xs = nn(hT, hot_s[0:C]).astype(BF16)
    xr = nn(hT, hot_r).astype(BF16)
    a0 = nn(w1T, jnp.concatenate([eT, xs, xr], axis=0))
    xT[0:H] = eT
    xT[H : 2 * H] = xs
    xT[2 * H : 3 * H] = xr

    for load in loads[7:]:
        load.wait()
    ceT[...] = nt(eye, ce_v[...]).astype(BF16)
    cnT = nt(eye, cn_v[...])
    n1b = n1[...].astype(BF16)
    n2b = n2[...].astype(BF16)
    n1T = nt(eye, n1b).astype(BF16)
    n2T = nt(eye, n2b).astype(BF16)
    w1b = w1[...].astype(BF16)
    w2b = w2[...].astype(BF16)
    slot = lax.broadcasted_iota(jnp.int32, (1, E), 1)
    gain_e = column_of(eg[...])
    gain_n = column_of(ng[...])
    gain_tile = across(gain_e, E)
    count = cnt[0, 0]

    for copy in ghost_out:
        copy.wait_recv()
    ghosts = jnp.concatenate([gs_recv[0], gs_recv[1], gs_recv[2], gs_recv[0]], axis=0)
    first_here = jnp.logical_and(lane < GQ, low)
    last_here = jnp.logical_and(lane >= 3 * GQ, jnp.logical_not(low))
    here = jnp.logical_or(middle, jnp.logical_or(first_here, last_here))
    ghost_T = jnp.where(here, nt(eye, ghosts), 0.0).astype(BF16)

    live = jnp.where(slot < count, 1.0, 0.0)

    xg = nn(ghost_T, hot[C:T]).astype(BF16)
    p, d = silu_parts(a0 + nn(w1s_T, xg))
    xT[H : 2 * H] += xg
    pT = p.astype(BF16)
    dsil[...] = d
    nh, e_rs = normed(nn(w2T, pT))
    nhat[...] = nh
    msg = (live * (eT.astype(F32) + live * (nh * gain_tile))).astype(BF16)
    agg = nt(msg, hot[T : T + C]).astype(BF16)

    yT = jnp.concatenate([hT, agg], axis=0)
    r, dr_ = silu_parts(nn(n1T, yT))
    r = r.astype(BF16)
    nh, rs = normed(nn(n2T, r))
    acc = folded(cnT * nh)
    ds = normed_back(cnT * across(gain_n, C), nh, rs).astype(BF16)
    dc = (nn(n2b, ds).astype(BF16).astype(F32) * dr_).astype(BF16)
    dyT = nn(n1b, dc).astype(BF16)
    dagg = dyT[H:]
    b_send[0 : 2 * H] = nt(yT, dc).astype(BF16)
    b_send[2 * H : 3 * H] = nt(r, ds).astype(BF16)
    b_send[3 * H :] = jnp.zeros((b_send.shape[0] - 3 * H, H), BF16)
    gain_n_row = row_of(acc)
    node_T = cnT + dyT[0:H].astype(F32)

    def shard(i):
        return pl.ds(pl.multiple_of(i * share, share), share)

    def push(src, dst, phase, to):
        pltpu.make_async_remote_copy(
            src_ref=src, dst_ref=dst, send_sem=psem_s.at[phase], recv_sem=psem_r.at[phase],
            device_id=to, device_id_type=MESH,
        ).start()

    def await_bytes(ref, sem):
        pltpu.make_async_copy(ref, ref, sem).wait()

    b_others = b_recv.at[pl.ds(0, group - 1)]
    b_levels = b_lift.at[pl.ds(0, depth - 1)]
    b_shares = b_all.at[pl.ds(0, group - 1)]

    each_member(lambda i, to: push(b_send.at[shard(i)], b_recv.at[mine], 0, to))
    b_recv[mine] = b_send[shard(mine)]

    g = ceT[...].astype(F32) + live * nn(dagg, hot[T : T + C])
    gT[...] = g
    dd = live * g
    nh = nhat[...]
    acc = folded(dd * nh)
    db = normed_back(dd * gain_tile, nh, e_rs).astype(BF16)
    dp = nn(w2b, db).astype(BF16).astype(F32)
    da = (dp * dsil[...]).astype(BF16)

    a_send[0 : 3 * H] = nt(xT[...], da).astype(BF16)
    a_send[3 * H : 4 * H] = nt(pT, db).astype(BF16)
    gain_row = lax.broadcasted_iota(jnp.int32, (GAIN_ROWS, H), 0)
    gains = jnp.where(gain_row == 0, row_of(acc), jnp.where(gain_row == 1, gain_n_row, 0.0))
    a_send[4 * H :] = gains.astype(BF16)

    wide = share + GAIN_ROWS
    wide_rows = pl.ds(last * share, wide)
    narrow = pl.ds(0, share)
    is_last = mine == last

    gain_rows = pl.ds(group * share, GAIN_ROWS)
    each_member(lambda i, to: push(a_send.at[shard(i)], a_recv.at[mine, narrow], 2, to))

    @pl.when(jnp.logical_not(is_last))
    def _():
        push(a_send.at[gain_rows], a_recv.at[mine, pl.ds(share, GAIN_ROWS)], 2, member(last))

    @pl.when(is_last)
    def _():
        a_recv[mine] = a_send[wide_rows]

    @pl.when(jnp.logical_not(is_last))
    def _():
        a_recv[mine, 0:share] = a_send[shard(mine)]

    s_all = nt(hot[...], da).astype(BF16)
    dghost = nt(s_all[C:T], w1b[H : 2 * H])
    gb_send[0] = (dghost[0:GQ] + dghost[3 * GQ : 4 * GQ]).astype(BF16)
    gb_send[1] = dghost[GQ : 2 * GQ].astype(BF16)
    gb_send[2] = dghost[2 * GQ : 3 * GQ].astype(BF16)
    ghost_back = [
        pltpu.make_async_remote_copy(
            src_ref=gb_send.at[k], dst_ref=gb_recv.at[k], send_sem=bsem_s.at[k], recv_sem=bsem_r.at[k],
            device_id=(to, core), device_id_type=MESH,
        )
        for k, to in enumerate((partner, right, left))
    ]
    for copy in ghost_back:
        copy.start()

    await_bytes(b_others, psem_r.at[0])
    b_lift[level] = jnp.sum(b_recv[...].astype(F32), axis=0).astype(BF16)
    each_level(lambda to: push(b_lift.at[level], b_lift.at[level], 1, to))

    dx = nn(w1b[0:H], da).astype(BF16).astype(F32)
    half_e = E // 2
    gedge[0:half_e] = (gT[:, 0:half_e] + dx[:, 0:half_e]).T

    @pl.when(is_last)
    def _():
        await_bytes(a_recv.at[pl.ds(0, group - 1)], psem_r.at[2])
        a_lift[level] = jnp.sum(a_recv[...].astype(F32), axis=0).astype(BF16)
        each_level(lambda to: push(a_lift.at[level], a_lift.at[level], 4, to))

    @pl.when(jnp.logical_not(is_last))
    def _():
        await_bytes(a_recv.at[pl.ds(0, group - 1), narrow], psem_r.at[2])
        a_lift[level, 0:share] = jnp.sum(a_recv[:, 0:share].astype(F32), axis=0).astype(BF16)
        each_level(lambda to: push(a_lift.at[level, narrow], a_lift.at[level, narrow], 4, to))

    await_bytes(b_levels, psem_r.at[1])
    b_all[mine] = (jnp.sum(b_lift[...].astype(F32), axis=0) * factor).astype(BF16)
    each_member(lambda i, to: push(b_all.at[mine], b_all.at[mine], 3, to))

    gedge[half_e:E] = (gT[:, half_e:E] + dx[:, half_e:E]).T
    own = nt(s_all[0:C], w1b[H : 2 * H]).astype(BF16).astype(F32)
    own = own + nt(s_all[T:], w1b[2 * H : 3 * H]).astype(BF16).astype(F32)
    gnode[...] = node_T.T + own

    @pl.when(is_last)
    def _():
        await_bytes(a_lift.at[pl.ds(0, depth - 1)], psem_r.at[4])
        total = (jnp.sum(a_lift[...].astype(F32), axis=0) * factor).astype(BF16)
        a_all[wide_rows] = total
        each_member(lambda i, to: push(a_all.at[wide_rows], a_all.at[wide_rows], 5, to))

    @pl.when(jnp.logical_not(is_last))
    def _():
        await_bytes(a_lift.at[pl.ds(0, depth - 1), narrow], psem_r.at[4])
        total = (jnp.sum(a_lift[:, 0:share].astype(F32), axis=0) * factor).astype(BF16)
        a_all[shard(mine)] = total
        each_member(lambda i, to: push(a_all.at[shard(mine)], a_all.at[shard(mine)], 5, to))

    for copy in ghost_back:
        copy.wait_recv()
    back = jnp.concatenate([gb_recv[0], gb_recv[1], gb_recv[2], gb_recv[0]], axis=0)
    gnode[...] += nn(hot_out, back)

    await_bytes(b_shares, psem_r.at[3])
    gn1[...] = b_all[0 : 2 * H // share].astype(F32).reshape(2 * H, H)
    gn2[...] = b_all[2 * H // share : 3 * H // share].astype(F32).reshape(H, H)

    for copy in ghost_out + ghost_back:
        copy.wait_send()
    await_bytes(b_others, psem_s.at[0])
    await_bytes(b_levels, psem_s.at[1])
    await_bytes(b_shares, psem_s.at[3])

    without_share = a_all.at[pl.ds(0, (group - 1) * share)]
    without_gains = a_all.at[pl.ds(0, (group - 1) * share + GAIN_ROWS)]

    @pl.when(is_last)
    def _():
        await_bytes(without_share, psem_s.at[2])
        await_bytes(a_lift.at[pl.ds(0, depth - 1)], psem_s.at[4])
        await_bytes(a_recv.at[pl.ds(0, group - 1)], psem_s.at[5])
        await_bytes(without_share, psem_r.at[5])

    @pl.when(jnp.logical_not(is_last))
    def _():
        await_bytes(without_gains, psem_s.at[2])
        await_bytes(a_lift.at[pl.ds(0, depth - 1), narrow], psem_s.at[4])
        await_bytes(a_recv.at[pl.ds(0, group - 1), narrow], psem_s.at[5])
        await_bytes(without_gains, psem_r.at[5])

    gw1[...] = a_all[0 : 3 * H].astype(F32)
    gw2[...] = a_all[3 * H : 4 * H].astype(F32)
    tail = a_all[4 * H : 4 * H + GAIN_ROWS].astype(F32)
    geg[...] = tail[0:1]
    gng[...] = tail[1:2]


def deliver(*refs):
    n = len(refs) // 2
    sem = refs[-1]
    pairs = []
    for i in range(n):
        src, dst = refs[i], refs[n + i]
        size = src.shape[0]
        if size > 512:
            cuts = [pl.ds(j * size // PIECES, size // PIECES) for j in range(PIECES)]
            pairs += [(src.at[c], dst.at[c]) for c in cuts]
        else:
            pairs.append((src, dst))
    copies = [pltpu.make_async_copy(src, dst, sem.at[i]) for i, (src, dst) in enumerate(pairs)]
    for copy in copies:
        copy.start()
    for copy in copies:
        copy.wait()


def on_device(
    plane, node_feat, edge_feat, cot_node, cot_edge, senders, receivers, send_rows, edge_count,
    edge_w1, edge_w2, edge_gain, node_w1, node_w2, node_gain,
):
    peers, dps = lax.axis_size("morton"), lax.axis_size("dp")
    C, H = node_feat.shape[1:]
    E = edge_feat.shape[1]
    GH = send_rows.shape[1]
    GQ = GH // 4
    T = C + GH
    group = plane * dps
    depth = peers // plane
    share = 4 * H // group
    factor = (dps * peers * E) ** -0.5
    vmem = pl.BlockSpec(memory_space=pltpu.VMEM)
    hbm = pl.BlockSpec(memory_space=pltpu.HBM)
    shape = jax.ShapeDtypeStruct
    dma = pltpu.SemaphoreType.DMA
    results = [
        shape((C, H), F32), shape((E, H), F32), shape((3 * H, H), F32), shape((H, H), F32),
        shape((1, H), F32), shape((2 * H, H), F32), shape((H, H), F32), shape((1, H), F32),
    ]
    args = [
        node_feat[0], send_rows, edge_feat[0], senders, receivers, edge_w1, edge_w2, edge_count,
        edge_gain.reshape(1, H), node_gain.reshape(1, H), node_w1, node_w2, cot_node[0], cot_edge[0],
    ]
    args = [a if a is edge_count else pltpu.with_memory_space_constraint(a, pltpu.HBM) for a in args]
    landing = [pltpu.VMEM(a.shape, a.dtype) for a in args]
    landing[7] = pltpu.SMEM((1, 1), jnp.int32)
    outs = pl.pallas_call(
        functools.partial(kernel, (peers, dps, plane, factor)),
        out_shape=results,
        in_specs=[hbm] * 14,
        out_specs=[vmem] * 8,
        scratch_shapes=landing + [
            dma((14,)),
            pltpu.VMEM((T + C, E), BF16), pltpu.VMEM((3 * H, E), BF16), pltpu.VMEM((H, E), BF16),
            pltpu.VMEM((H, E), F32), pltpu.VMEM((H, E), F32), pltpu.VMEM((H, E), F32),
            pltpu.VMEM((3, GQ, H), BF16), pltpu.VMEM((3, GQ, H), BF16),
            pltpu.VMEM((3, GQ, H), BF16), pltpu.VMEM((3, GQ, H), BF16),
            dma((3,)), dma((3,)), dma((3,)), dma((3,)),
            pltpu.VMEM((4 * H + GAIN_ROWS, H), BF16), pltpu.VMEM((group, share + GAIN_ROWS, H), BF16),
            pltpu.VMEM((depth, share + GAIN_ROWS, H), BF16), pltpu.VMEM((4 * H + GAIN_ROWS, H), BF16),
            pltpu.VMEM((4 * H, H), BF16), pltpu.VMEM((group, share, H), BF16),
            pltpu.VMEM((depth, share, H), BF16), pltpu.VMEM((group, share, H), BF16),
            dma((6,)), dma((6,)),
        ],
        compiler_params=pltpu.CompilerParams(
            collective_id=0, has_side_effects=True, vmem_limit_bytes=40 * 1024 * 1024
        ),
    )(*args)
    outs = [pltpu.with_memory_space_constraint(a, pltpu.VMEM) for a in outs]
    outs = pl.pallas_call(
        deliver,
        out_shape=results,
        in_specs=[vmem] * 8,
        out_specs=[hbm] * 8,
        scratch_shapes=[dma((7 + PIECES,))],
    )(*outs)
    return (
        outs[0][None], outs[1][None], outs[2], outs[3], outs[4].reshape(H), outs[5], outs[6], outs[7].reshape(H)
    )


def solution(mesh):
    cells = P("dp", "morton", None)
    flat = P("dp", "morton")
    plane = min(16, mesh.shape["morton"] // 2)
    return jax.shard_map(
        functools.partial(on_device, plane),
        mesh=mesh,
        in_specs=(cells, cells, cells, cells, flat, flat, flat, flat, P(), P(), P(), P(), P(), P()),
        out_specs=(cells, cells, P(), P(), P(), P(), P(), P()),
        check_vma=False,
    )
```

```python
import functools

import jax
import jax.numpy as jnp
from jax import lax
from jax.experimental import pallas as pl
from jax.experimental.pallas import tpu as pltpu
from jax.sharding import PartitionSpec as P

MESH = pl.DeviceIdType.MESH
F32 = jnp.float32
BF16 = jnp.bfloat16
GAIN_ROWS = 16


SIDE = 4
PIECES = 4


def ring(offset, size):
    return min(offset, size - offset)


def farthest_first(plane, dps):
    steps = [(ox, oy, oc) for ox in range(plane // SIDE) for oy in range(SIDE) for oc in range(dps)]
    return sorted(steps[1:], key=lambda o: -(ring(o[0], SIDE) + ring(o[1], SIDE)))


def nn(a, b):
    return lax.dot_general(a, b, (((1,), (0,)), ((), ())), preferred_element_type=F32)


def nt(a, b):
    return lax.dot_general(a, b, (((1,), (1,)), ((), ())), preferred_element_type=F32)


def one_hot(row, depth):
    spot = lax.broadcasted_iota(jnp.int32, (depth, row.shape[1]), 0)
    return jnp.where(spot == row, 1.0, 0.0).astype(BF16)


def sigmoid(a):
    return 0.5 * jnp.tanh(0.5 * a) + 0.5


def silu_parts(a):
    s = sigmoid(a)
    return a * s, s * (1.0 + a * (1.0 - s))


def column_of(row):
    return jnp.broadcast_to(row, (row.shape[1], row.shape[1])).T


def across(column, width):
    return jnp.concatenate([column] * (width // column.shape[1]), axis=1)


def folded(values):
    step = values.shape[0]
    return sum(values[:, i : i + step] for i in range(0, values.shape[1], step))


def row_of(partial):
    return jnp.sum(partial.T, axis=0, keepdims=True)


def normed(b):
    center = b - jnp.mean(b, axis=0, keepdims=True)
    spread = jnp.mean(center * center, axis=0, keepdims=True)
    rs = lax.rsqrt(spread + 1e-05)
    return center * rs, rs


def normed_back(dn, nh, rs):
    m1 = jnp.mean(dn, axis=0, keepdims=True)
    m2 = jnp.mean(dn * nh, axis=0, keepdims=True)
    return rs * (dn - m1 - nh * m2)


def kernel(
    sizes,
    node_hbm, rows_hbm, edge_hbm, snd_hbm, rcv_hbm, w1_hbm, w2_hbm, cnt_hbm,
    eg_hbm, ng_hbm, n1_hbm, n2_hbm, cotn_hbm, cote_hbm,
    gnode, gedge, gw1, gw2, geg, gn1, gn2, gng,
    h_v, rows, e_v, snd, rcv, w1, w2, cnt, eg, ng, n1, n2, cn_v, ce_v, in_sem,
    hot, xT, ceT, live_eT, live_gain, dsil, nhat, gT,
    gs_send, gs_recv, gb_send, gb_recv, gsem_s, gsem_r, bsem_s, bsem_r,
    a_send, a_recv, a_lift, a_all, b_send, b_recv, b_lift, b_all, psem_s, psem_r,
):
    peers, dps, plane, factor = sizes
    group = plane * dps
    depth = peers // plane
    C, H = h_v.shape
    E = e_v.shape[0]
    GH = rows.shape[1]
    GQ = GH // 4
    T = C + GH
    share = b_recv.shape[1]
    half = peers // 2
    last = group - 1

    m = lax.axis_index("morton")
    core = lax.axis_index("dp")
    level = m // plane
    mine = (m % plane) * dps + core
    low = m < half
    partner = lax.rem(m + half, peers)
    right = lax.rem(m + 1, peers)
    left = lax.rem(m + peers - 1, peers)

    def member(i):
        return (level * plane + i // dps, i % dps)

    mx = (m % plane) // SIDE
    my = m % SIDE

    def above(z):
        return (z * plane + m % plane, core)

    barrier = pltpu.get_barrier_semaphore()

    def greet(to):
        pl.semaphore_signal(barrier, inc=1, device_id=to, device_id_type=MESH)

    def each_member(act):
        for ox, oy, oc in farthest_first(plane, dps):
            column = lax.rem(mx + ox, SIDE) * SIDE + lax.rem(my + oy, SIDE)
            other = lax.rem(core + oc, dps)
            act(column * dps + other, (level * plane + column, other))

    def each_level(act):
        for o in sorted(range(1, depth), key=lambda o: -ring(o, depth)):
            act(above(lax.rem(level + o, depth)))

    greet((partner, core))
    sources = (
        node_hbm, rows_hbm, edge_hbm, snd_hbm, rcv_hbm, w1_hbm, w2_hbm, cnt_hbm,
        eg_hbm, ng_hbm, n1_hbm, n2_hbm, cotn_hbm, cote_hbm,
    )
    places = (h_v, rows, e_v, snd, rcv, w1, w2, cnt, eg, ng, n1, n2, cn_v, ce_v)
    loads = [
        pltpu.make_async_copy(src, dst, in_sem.at[i]) for i, (src, dst) in enumerate(zip(sources, places))
    ]
    loads[0].start()
    loads[1].start()
    greet((left, core))
    greet((right, core))
    for load in loads[2:]:
        load.start()

    each_level(greet)
    each_member(lambda i, to: greet(to))

    eye_r = lax.broadcasted_iota(jnp.int32, (H, H), 0)
    eye_c = lax.broadcasted_iota(jnp.int32, (H, H), 1)
    eye = jnp.where(eye_r == eye_c, 1.0, 0.0).astype(BF16)

    lane = lax.broadcasted_iota(jnp.int32, (1, GH), 1)
    first_used = jnp.logical_and(lane < GQ, jnp.logical_not(low))
    last_used = jnp.logical_and(lane >= 3 * GQ, low)
    middle = jnp.logical_and(lane >= GQ, lane < 3 * GQ)
    used = jnp.logical_or(middle, jnp.logical_or(first_used, last_used))
    loads[0].wait()
    loads[1].wait()
    hot_out = one_hot(jnp.where(used, rows[...], -1), C)

    hT = nt(eye, h_v[...]).astype(BF16)
    picked = nn(hT, hot_out).T
    gs_send[0] = (picked[0:GQ] + picked[3 * GQ : 4 * GQ]).astype(BF16)
    gs_send[1] = picked[GQ : 2 * GQ].astype(BF16)
    gs_send[2] = picked[2 * GQ : 3 * GQ].astype(BF16)

    pl.semaphore_wait(barrier, (group - 1) + (depth - 1) + 3)

    ghost_out = [
        pltpu.make_async_remote_copy(
            src_ref=gs_send.at[k], dst_ref=gs_recv.at[k], send_sem=gsem_s.at[k], recv_sem=gsem_r.at[k],
            device_id=(to, core), device_id_type=MESH,
        )
        for k, to in enumerate((partner, left, right))
    ]
    for copy in ghost_out:
        copy.start()

    for load in loads[2:7]:
        load.wait()
    w1T = nt(eye, w1[...].astype(BF16)).astype(BF16)
    w2T = nt(eye, w2[...].astype(BF16)).astype(BF16)
    w1s_T = w1T[:, H : 2 * H]

    hot_s = one_hot(snd[...], T)
    hot_r = one_hot(rcv[...], C)
    hot[0:T] = hot_s
    hot[T : T + C] = hot_r
    eT = nt(eye, e_v[...]).astype(BF16)
    xs = nn(hT, hot_s[0:C]).astype(BF16)
    xr = nn(hT, hot_r).astype(BF16)
    a0 = nn(w1T, jnp.concatenate([eT, xs, xr], axis=0))
    xT[0:H] = eT
    xT[2 * H : 3 * H] = xr

    for load in loads[7:]:
        load.wait()
    ceT[...] = nt(eye, ce_v[...]).astype(BF16)
    cnT = nt(eye, cn_v[...])
    n1b = n1[...].astype(BF16)
    n2b = n2[...].astype(BF16)
    n1T = nt(eye, n1b).astype(BF16)
    n2T = nt(eye, n2b).astype(BF16)
    w1b = w1[...].astype(BF16)
    w2b = w2[...].astype(BF16)
    slot = lax.broadcasted_iota(jnp.int32, (1, E), 1)
    gain_e = column_of(eg[...])
    gain_n = column_of(ng[...])
    gain_tile = across(gain_e, E)
    count = cnt[0, 0]

    live = jnp.where(slot < count, 1.0, 0.0)
    live_eT[...] = live * eT.astype(F32)
    live_gain[...] = live * gain_tile

    for copy in ghost_out:
        copy.wait_recv()
    ghosts = jnp.concatenate([gs_recv[0], gs_recv[1], gs_recv[2], gs_recv[0]], axis=0)
    first_here = jnp.logical_and(lane < GQ, low)
    last_here = jnp.logical_and(lane >= 3 * GQ, jnp.logical_not(low))
    here = jnp.logical_or(middle, jnp.logical_or(first_here, last_here))
    ghost_T = jnp.where(here, nt(eye, ghosts), 0.0).astype(BF16)

    xg = nn(ghost_T, hot[C:T])
    p, d = silu_parts(a0 + nn(w1s_T, xg.astype(BF16)))
    xT[H : 2 * H] = (xs.astype(F32) + xg).astype(BF16)
    pT = p.astype(BF16)
    dsil[...] = d
    nh, e_rs = normed(nn(w2T, pT))
    nhat[...] = nh
    msg = (live_eT[...] + live_gain[...] * nh).astype(BF16)
    agg = nt(msg, hot[T : T + C]).astype(BF16)

    yT = jnp.concatenate([hT, agg], axis=0)
    r, dr_ = silu_parts(nn(n1T, yT))
    r = r.astype(BF16)
    nh, rs = normed(nn(n2T, r))
    acc = folded(cnT * nh)
    ds = normed_back(cnT * across(gain_n, C), nh, rs).astype(BF16)
    dc = (nn(n2b, ds).astype(BF16).astype(F32) * dr_).astype(BF16)
    dyT = nn(n1b, dc).astype(BF16)
    dagg = dyT[H:]
    b_send[0 : 2 * H] = nt(yT, dc).astype(BF16)
    b_send[2 * H : 3 * H] = nt(r, ds).astype(BF16)
    b_send[3 * H :] = jnp.zeros((b_send.shape[0] - 3 * H, H), BF16)
    gain_n_row = row_of(acc)
    node_T = cnT + dyT[0:H].astype(F32)

    def shard(i):
        return pl.ds(pl.multiple_of(i * share, share), share)

    def push(src, dst, phase, to):
        pltpu.make_async_remote_copy(
            src_ref=src, dst_ref=dst, send_sem=psem_s.at[phase], recv_sem=psem_r.at[phase],
            device_id=to, device_id_type=MESH,
        ).start()

    def await_bytes(ref, sem):
        pltpu.make_async_copy(ref, ref, sem).wait()

    b_others = b_recv.at[pl.ds(0, group - 1)]
    b_levels = b_lift.at[pl.ds(0, depth - 1)]
    b_shares = b_all.at[pl.ds(0, group - 1)]

    each_member(lambda i, to: push(b_send.at[shard(i)], b_recv.at[mine], 0, to))
    b_recv[mine] = b_send[shard(mine)]

    g = ceT[...].astype(F32) + live * nn(dagg, hot[T : T + C])
    gT[...] = g
    dd = live * g
    nh = nhat[...]
    acc = folded(dd * nh)
    db = normed_back(live_gain[...] * g, nh, e_rs).astype(BF16)
    dp = nn(w2b, db).astype(BF16).astype(F32)
    da = (dp * dsil[...]).astype(BF16)

    a_send[0 : 3 * H] = nt(da, xT[...]).T.astype(BF16)
    a_send[3 * H : 4 * H] = nt(pT, db).astype(BF16)
    gain_row = lax.broadcasted_iota(jnp.int32, (GAIN_ROWS, H), 0)
    gains = jnp.where(gain_row == 0, row_of(acc), jnp.where(gain_row == 1, gain_n_row, 0.0))
    a_send[4 * H :] = gains.astype(BF16)

    wide = share + GAIN_ROWS
    wide_rows = pl.ds(last * share, wide)
    narrow = pl.ds(0, share)
    is_last = mine == last

    gain_rows = pl.ds(group * share, GAIN_ROWS)
    each_member(lambda i, to: push(a_send.at[shard(i)], a_recv.at[mine, narrow], 2, to))

    @pl.when(jnp.logical_not(is_last))
    def _():
        push(a_send.at[gain_rows], a_recv.at[mine, pl.ds(share, GAIN_ROWS)], 2, member(last))

    @pl.when(is_last)
    def _():
        a_recv[mine] = a_send[wide_rows]

    @pl.when(jnp.logical_not(is_last))
    def _():
        a_recv[mine, 0:share] = a_send[shard(mine)]

    s_T = nt(da, hot[...]).astype(BF16)
    dghost = nn(w1b[H : 2 * H], s_T[:, C:T]).T
    gb_send[0] = (dghost[0:GQ] + dghost[3 * GQ : 4 * GQ]).astype(BF16)
    gb_send[1] = dghost[GQ : 2 * GQ].astype(BF16)
    gb_send[2] = dghost[2 * GQ : 3 * GQ].astype(BF16)
    ghost_back = [
        pltpu.make_async_remote_copy(
            src_ref=gb_send.at[k], dst_ref=gb_recv.at[k], send_sem=bsem_s.at[k], recv_sem=bsem_r.at[k],
            device_id=(to, core), device_id_type=MESH,
        )
        for k, to in enumerate((partner, right, left))
    ]
    for copy in ghost_back:
        copy.start()

    await_bytes(b_others, psem_r.at[0])
    b_lift[level] = jnp.sum(b_recv[...].astype(F32), axis=0).astype(BF16)
    each_level(lambda to: push(b_lift.at[level], b_lift.at[level], 1, to))

    dx = nn(w1b[0:H], da).astype(BF16).astype(F32)
    half_e = E // 2
    gedge[0:half_e] = (gT[:, 0:half_e] + dx[:, 0:half_e]).T

    @pl.when(is_last)
    def _():
        await_bytes(a_recv.at[pl.ds(0, group - 1)], psem_r.at[2])
        a_lift[level] = jnp.sum(a_recv[...].astype(F32), axis=0).astype(BF16)
        each_level(lambda to: push(a_lift.at[level], a_lift.at[level], 4, to))

    @pl.when(jnp.logical_not(is_last))
    def _():
        await_bytes(a_recv.at[pl.ds(0, group - 1), narrow], psem_r.at[2])
        a_lift[level, 0:share] = jnp.sum(a_recv[:, 0:share].astype(F32), axis=0).astype(BF16)
        each_level(lambda to: push(a_lift.at[level, narrow], a_lift.at[level, narrow], 4, to))

    await_bytes(b_levels, psem_r.at[1])
    b_all[mine] = (jnp.sum(b_lift[...].astype(F32), axis=0) * factor).astype(BF16)
    each_member(lambda i, to: push(b_all.at[mine], b_all.at[mine], 3, to))

    gedge[half_e:E] = (gT[:, half_e:E] + dx[:, half_e:E]).T
    own = nn(w1b[H : 2 * H], s_T[:, 0:C]) + nn(w1b[2 * H : 3 * H], s_T[:, T:])
    gnode[...] = (node_T + own).T

    @pl.when(is_last)
    def _():
        await_bytes(a_lift.at[pl.ds(0, depth - 1)], psem_r.at[4])
        total = (jnp.sum(a_lift[...].astype(F32), axis=0) * factor).astype(BF16)
        a_all[wide_rows] = total
        each_member(lambda i, to: push(a_all.at[wide_rows], a_all.at[wide_rows], 5, to))

    @pl.when(jnp.logical_not(is_last))
    def _():
        await_bytes(a_lift.at[pl.ds(0, depth - 1), narrow], psem_r.at[4])
        total = (jnp.sum(a_lift[:, 0:share].astype(F32), axis=0) * factor).astype(BF16)
        a_all[shard(mine)] = total
        each_member(lambda i, to: push(a_all.at[shard(mine)], a_all.at[shard(mine)], 5, to))

    for copy in ghost_back:
        copy.wait_recv()
    back = jnp.concatenate([gb_recv[0], gb_recv[1], gb_recv[2], gb_recv[0]], axis=0)
    gnode[...] += nn(hot_out, back)

    await_bytes(b_shares, psem_r.at[3])
    gn1[...] = b_all[0 : 2 * H // share].astype(F32).reshape(2 * H, H)
    gn2[...] = b_all[2 * H // share : 3 * H // share].astype(F32).reshape(H, H)

    for copy in ghost_out + ghost_back:
        copy.wait_send()
    await_bytes(b_others, psem_s.at[0])
    await_bytes(b_levels, psem_s.at[1])
    await_bytes(b_shares, psem_s.at[3])

    without_share = a_all.at[pl.ds(0, (group - 1) * share)]
    without_gains = a_all.at[pl.ds(0, (group - 1) * share + GAIN_ROWS)]

    @pl.when(is_last)
    def _():
        await_bytes(without_share, psem_s.at[2])
        await_bytes(a_lift.at[pl.ds(0, depth - 1)], psem_s.at[4])
        await_bytes(a_recv.at[pl.ds(0, group - 1)], psem_s.at[5])
        await_bytes(without_share, psem_r.at[5])

    @pl.when(jnp.logical_not(is_last))
    def _():
        await_bytes(without_gains, psem_s.at[2])
        await_bytes(a_lift.at[pl.ds(0, depth - 1), narrow], psem_s.at[4])
        await_bytes(a_recv.at[pl.ds(0, group - 1), narrow], psem_s.at[5])
        await_bytes(without_gains, psem_r.at[5])

    gw1[...] = a_all[0 : 3 * H].astype(F32)
    gw2[...] = a_all[3 * H : 4 * H].astype(F32)
    tail = a_all[4 * H : 4 * H + GAIN_ROWS].astype(F32)
    geg[...] = tail[0:1]
    gng[...] = tail[1:2]


def deliver(*refs):
    n = len(refs) // 2
    sem = refs[-1]
    pairs = []
    for i in range(n):
        src, dst = refs[i], refs[n + i]
        size = src.shape[0]
        if size > 512:
            cuts = [pl.ds(j * size // PIECES, size // PIECES) for j in range(PIECES)]
            pairs += [(src.at[c], dst.at[c]) for c in cuts]
        else:
            pairs.append((src, dst))
    copies = [pltpu.make_async_copy(src, dst, sem.at[i]) for i, (src, dst) in enumerate(pairs)]
    for copy in copies:
        copy.start()
    for copy in copies:
        copy.wait()


def on_device(
    plane, node_feat, edge_feat, cot_node, cot_edge, senders, receivers, send_rows, edge_count,
    edge_w1, edge_w2, edge_gain, node_w1, node_w2, node_gain,
):
    peers, dps = lax.axis_size("morton"), lax.axis_size("dp")
    C, H = node_feat.shape[1:]
    E = edge_feat.shape[1]
    GH = send_rows.shape[1]
    GQ = GH // 4
    T = C + GH
    group = plane * dps
    depth = peers // plane
    share = 4 * H // group
    factor = (dps * peers * E) ** -0.5
    vmem = pl.BlockSpec(memory_space=pltpu.VMEM)
    hbm = pl.BlockSpec(memory_space=pltpu.HBM)
    shape = jax.ShapeDtypeStruct
    dma = pltpu.SemaphoreType.DMA
    results = [
        shape((C, H), F32), shape((E, H), F32), shape((3 * H, H), F32), shape((H, H), F32),
        shape((1, H), F32), shape((2 * H, H), F32), shape((H, H), F32), shape((1, H), F32),
    ]
    args = [
        node_feat[0], send_rows, edge_feat[0], senders, receivers, edge_w1, edge_w2, edge_count,
        edge_gain.reshape(1, H), node_gain.reshape(1, H), node_w1, node_w2, cot_node[0], cot_edge[0],
    ]
    args = [a if a is edge_count else pltpu.with_memory_space_constraint(a, pltpu.HBM) for a in args]
    landing = [pltpu.VMEM(a.shape, a.dtype) for a in args]
    landing[7] = pltpu.SMEM((1, 1), jnp.int32)
    outs = pl.pallas_call(
        functools.partial(kernel, (peers, dps, plane, factor)),
        out_shape=results,
        in_specs=[hbm] * 14,
        out_specs=[vmem] * 8,
        scratch_shapes=landing + [
            dma((14,)),
            pltpu.VMEM((T + C, E), BF16), pltpu.VMEM((3 * H, E), BF16), pltpu.VMEM((H, E), BF16),
            pltpu.VMEM((H, E), F32), pltpu.VMEM((H, E), F32),
            pltpu.VMEM((H, E), F32), pltpu.VMEM((H, E), F32), pltpu.VMEM((H, E), F32),
            pltpu.VMEM((3, GQ, H), BF16), pltpu.VMEM((3, GQ, H), BF16),
            pltpu.VMEM((3, GQ, H), BF16), pltpu.VMEM((3, GQ, H), BF16),
            dma((3,)), dma((3,)), dma((3,)), dma((3,)),
            pltpu.VMEM((4 * H + GAIN_ROWS, H), BF16), pltpu.VMEM((group, share + GAIN_ROWS, H), BF16),
            pltpu.VMEM((depth, share + GAIN_ROWS, H), BF16), pltpu.VMEM((4 * H + GAIN_ROWS, H), BF16),
            pltpu.VMEM((4 * H, H), BF16), pltpu.VMEM((group, share, H), BF16),
            pltpu.VMEM((depth, share, H), BF16), pltpu.VMEM((group, share, H), BF16),
            dma((6,)), dma((6,)),
        ],
        compiler_params=pltpu.CompilerParams(
            collective_id=0, has_side_effects=True, vmem_limit_bytes=40 * 1024 * 1024
        ),
    )(*args)
    outs = [pltpu.with_memory_space_constraint(a, pltpu.VMEM) for a in outs]
    outs = pl.pallas_call(
        deliver,
        out_shape=results,
        in_specs=[vmem] * 8,
        out_specs=[hbm] * 8,
        scratch_shapes=[dma((7 + PIECES,))],
    )(*outs)
    return (
        outs[0][None], outs[1][None], outs[2], outs[3], outs[4].reshape(H), outs[5], outs[6], outs[7].reshape(H)
    )


def solution(mesh):
    cells = P("dp", "morton", None)
    flat = P("dp", "morton")
    plane = min(16, mesh.shape["morton"] // 2)
    return jax.shard_map(
        functools.partial(on_device, plane),
        mesh=mesh,
        in_specs=(cells, cells, cells, cells, flat, flat, flat, flat, P(), P(), P(), P(), P(), P()),
        out_specs=(cells, cells, P(), P(), P(), P(), P(), P()),
        check_vma=False,
    )
```

```python
import functools

import jax
import jax.numpy as jnp
from jax import lax
from jax.experimental import pallas as pl
from jax.experimental.pallas import tpu as pltpu
from jax.sharding import PartitionSpec as P

MESH = pl.DeviceIdType.MESH
F32 = jnp.float32
BF16 = jnp.bfloat16
GAIN_ROWS = 16


SIDE = 4
PIECES = 4


def ring(offset, size):
    return min(offset, size - offset)


def farthest_first(plane, dps):
    steps = [(ox, oy, oc) for ox in range(plane // SIDE) for oy in range(SIDE) for oc in range(dps)]
    return sorted(steps[1:], key=lambda o: -(ring(o[0], SIDE) + ring(o[1], SIDE)))


def nn(a, b):
    return lax.dot_general(a, b, (((1,), (0,)), ((), ())), preferred_element_type=F32)


def nt(a, b):
    return lax.dot_general(a, b, (((1,), (1,)), ((), ())), preferred_element_type=F32)


def one_hot(row, depth):
    spot = lax.broadcasted_iota(jnp.int32, (depth, row.shape[1]), 0)
    return jnp.where(spot == row, 1.0, 0.0).astype(BF16)


def sigmoid(a):
    return 0.5 * jnp.tanh(0.5 * a) + 0.5


def silu_parts(a):
    s = sigmoid(a)
    return a * s, s * (1.0 + a * (1.0 - s))


def column_of(row):
    return jnp.broadcast_to(row, (row.shape[1], row.shape[1])).T


def across(column, width):
    return jnp.concatenate([column] * (width // column.shape[1]), axis=1)


def folded(values):
    step = values.shape[0]
    return sum(values[:, i : i + step] for i in range(0, values.shape[1], step))


def row_of(partial):
    return jnp.sum(partial.T, axis=0, keepdims=True)


def normed(b):
    center = b - jnp.mean(b, axis=0, keepdims=True)
    spread = jnp.mean(center * center, axis=0, keepdims=True)
    rs = lax.rsqrt(spread + 1e-05)
    return center * rs, rs


def normed_back(dn, nh, rs):
    m1 = jnp.mean(dn, axis=0, keepdims=True)
    m2 = jnp.mean(dn * nh, axis=0, keepdims=True)
    return rs * (dn - m1 - nh * m2)


def kernel(
    sizes,
    node_hbm, rows_hbm, edge_hbm, snd_hbm, rcv_hbm, w1_hbm, w2_hbm, cnt_hbm,
    eg_hbm, ng_hbm, n1_hbm, n2_hbm, cotn_hbm, cote_hbm,
    gnode, gedge, gw1, gw2, geg, gn1, gn2, gng,
    h_v, rows, e_v, snd, rcv, w1, w2, cnt, eg, ng, n1, n2, cn_v, ce_v, in_sem,
    hot, xT, ceT, live_eT, live_gain, dsil, nhat, gT,
    gs_send, gs_recv, gb_send, gb_recv, gsem_s, gsem_r, bsem_s, bsem_r,
    a_send, a_recv, a_lift, a_all, b_send, b_recv, b_lift, b_all, psem_s, psem_r,
):
    peers, dps, plane, factor = sizes
    group = plane * dps
    depth = peers // plane
    C, H = h_v.shape
    E = e_v.shape[0]
    GH = rows.shape[1]
    GQ = GH // 4
    T = C + GH
    share = b_recv.shape[1]
    half = peers // 2
    last = group - 1

    m = lax.axis_index("morton")
    core = lax.axis_index("dp")
    level = m // plane
    mine = (m % plane) * dps + core
    low = m < half
    partner = lax.rem(m + half, peers)
    right = lax.rem(m + 1, peers)
    left = lax.rem(m + peers - 1, peers)

    def member(i):
        return (level * plane + i // dps, i % dps)

    mx = (m % plane) // SIDE
    my = m % SIDE

    def above(z):
        return (z * plane + m % plane, core)

    barrier = pltpu.get_barrier_semaphore()

    def greet(to):
        pl.semaphore_signal(barrier, inc=1, device_id=to, device_id_type=MESH)

    def each_member(act):
        for ox, oy, oc in farthest_first(plane, dps):
            column = lax.rem(mx + ox, SIDE) * SIDE + lax.rem(my + oy, SIDE)
            other = lax.rem(core + oc, dps)
            act(column * dps + other, (level * plane + column, other))

    def each_level(act):
        for o in sorted(range(1, depth), key=lambda o: -ring(o, depth)):
            act(above(lax.rem(level + o, depth)))

    greet((partner, core))
    sources = (
        node_hbm, rows_hbm, edge_hbm, snd_hbm, rcv_hbm, w1_hbm, w2_hbm, cnt_hbm,
        eg_hbm, ng_hbm, n1_hbm, n2_hbm, cotn_hbm, cote_hbm,
    )
    places = (h_v, rows, e_v, snd, rcv, w1, w2, cnt, eg, ng, n1, n2, cn_v, ce_v)
    loads = [
        pltpu.make_async_copy(src, dst, in_sem.at[i]) for i, (src, dst) in enumerate(zip(sources, places))
    ]
    loads[0].start()
    loads[1].start()
    greet((left, core))
    greet((right, core))
    for load in loads[2:]:
        load.start()

    for o in range(1, depth):
        if o != depth // 2:
            greet(above(lax.rem(level + o, depth)))
    each_member(lambda i, to: greet(to))

    eye_r = lax.broadcasted_iota(jnp.int32, (H, H), 0)
    eye_c = lax.broadcasted_iota(jnp.int32, (H, H), 1)
    eye = jnp.where(eye_r == eye_c, 1.0, 0.0).astype(BF16)

    lane = lax.broadcasted_iota(jnp.int32, (1, GH), 1)
    first_used = jnp.logical_and(lane < GQ, jnp.logical_not(low))
    last_used = jnp.logical_and(lane >= 3 * GQ, low)
    middle = jnp.logical_and(lane >= GQ, lane < 3 * GQ)
    used = jnp.logical_or(middle, jnp.logical_or(first_used, last_used))
    loads[0].wait()
    loads[1].wait()
    hot_out = one_hot(jnp.where(used, rows[...], -1), C)

    hT = nt(eye, h_v[...]).astype(BF16)
    picked = nn(hT, hot_out).T
    gs_send[0] = (picked[0:GQ] + picked[3 * GQ : 4 * GQ]).astype(BF16)
    gs_send[1] = picked[GQ : 2 * GQ].astype(BF16)
    gs_send[2] = picked[2 * GQ : 3 * GQ].astype(BF16)

    pl.semaphore_wait(barrier, (group - 1) + (depth - 2) + 3)

    ghost_out = [
        pltpu.make_async_remote_copy(
            src_ref=gs_send.at[k], dst_ref=gs_recv.at[k], send_sem=gsem_s.at[k], recv_sem=gsem_r.at[k],
            device_id=(to, core), device_id_type=MESH,
        )
        for k, to in enumerate((partner, left, right))
    ]
    for copy in ghost_out:
        copy.start()

    for load in loads[2:7]:
        load.wait()
    w1T = nt(eye, w1[...].astype(BF16)).astype(BF16)
    w2T = nt(eye, w2[...].astype(BF16)).astype(BF16)
    w1s_T = w1T[:, H : 2 * H]

    hot_s = one_hot(snd[...], T)
    hot_r = one_hot(rcv[...], C)
    hot[0:T] = hot_s
    hot[T : T + C] = hot_r
    eT = nt(eye, e_v[...]).astype(BF16)
    xs = nn(hT, hot_s[0:C]).astype(BF16)
    xr = nn(hT, hot_r).astype(BF16)
    a0 = nn(w1T, jnp.concatenate([eT, xs, xr], axis=0))
    xT[0:H] = eT
    xT[2 * H : 3 * H] = xr

    for load in loads[7:]:
        load.wait()
    ceT[...] = nt(eye, ce_v[...]).astype(BF16)
    cnT = nt(eye, cn_v[...])
    n1b = n1[...].astype(BF16)
    n2b = n2[...].astype(BF16)
    n1T = nt(eye, n1b).astype(BF16)
    n2T = nt(eye, n2b).astype(BF16)
    w1b = w1[...].astype(BF16)
    w2b = w2[...].astype(BF16)
    slot = lax.broadcasted_iota(jnp.int32, (1, E), 1)
    gain_e = column_of(eg[...])
    gain_n = column_of(ng[...])
    gain_tile = across(gain_e, E)
    count = cnt[0, 0]

    live = jnp.where(slot < count, 1.0, 0.0)
    live_eT[...] = live * eT.astype(F32)
    live_gain[...] = live * gain_tile

    for copy in ghost_out:
        copy.wait_recv()
    ghosts = jnp.concatenate([gs_recv[0], gs_recv[1], gs_recv[2], gs_recv[0]], axis=0)
    first_here = jnp.logical_and(lane < GQ, low)
    last_here = jnp.logical_and(lane >= 3 * GQ, jnp.logical_not(low))
    here = jnp.logical_or(middle, jnp.logical_or(first_here, last_here))
    ghost_T = jnp.where(here, nt(eye, ghosts), 0.0).astype(BF16)

    xg = nn(ghost_T, hot[C:T])
    p, d = silu_parts(a0 + nn(w1s_T, xg.astype(BF16)))
    xT[H : 2 * H] = (xs.astype(F32) + xg).astype(BF16)
    pT = p.astype(BF16)
    dsil[...] = d
    nh, e_rs = normed(nn(w2T, pT))
    nhat[...] = nh
    msg = (live_eT[...] + live_gain[...] * nh).astype(BF16)
    agg = nt(msg, hot[T : T + C]).astype(BF16)

    yT = jnp.concatenate([hT, agg], axis=0)
    r, dr_ = silu_parts(nn(n1T, yT))
    r = r.astype(BF16)
    nh, rs = normed(nn(n2T, r))
    acc = folded(cnT * nh)
    ds = normed_back(cnT * across(gain_n, C), nh, rs).astype(BF16)
    dc = (nn(n2b, ds).astype(BF16).astype(F32) * dr_).astype(BF16)
    dyT = nn(n1b, dc).astype(BF16)
    dagg = dyT[H:]
    b_send[0 : 2 * H] = nt(yT, dc).astype(BF16)
    b_send[2 * H : 3 * H] = nt(r, ds).astype(BF16)
    b_send[3 * H :] = jnp.zeros((b_send.shape[0] - 3 * H, H), BF16)
    gain_n_row = row_of(acc)
    node_T = cnT + dyT[0:H].astype(F32)

    def shard(i):
        return pl.ds(pl.multiple_of(i * share, share), share)

    def push(src, dst, phase, to):
        pltpu.make_async_remote_copy(
            src_ref=src, dst_ref=dst, send_sem=psem_s.at[phase], recv_sem=psem_r.at[phase],
            device_id=to, device_id_type=MESH,
        ).start()

    def await_bytes(ref, sem):
        pltpu.make_async_copy(ref, ref, sem).wait()

    b_others = b_recv.at[pl.ds(0, group - 1)]
    b_levels = b_lift.at[pl.ds(0, depth - 1)]
    b_shares = b_all.at[pl.ds(0, group - 1)]

    each_member(lambda i, to: push(b_send.at[shard(i)], b_recv.at[mine], 0, to))
    b_recv[mine] = b_send[shard(mine)]

    g = ceT[...].astype(F32) + live * nn(dagg, hot[T : T + C])
    gT[...] = g
    dd = live * g
    nh = nhat[...]
    acc = folded(dd * nh)
    db = normed_back(live_gain[...] * g, nh, e_rs).astype(BF16)
    dp = nn(w2b, db).astype(BF16).astype(F32)
    da = (dp * dsil[...]).astype(BF16)

    a_send[0 : 3 * H] = nt(da, xT[...]).T.astype(BF16)
    a_send[3 * H : 4 * H] = nt(pT, db).astype(BF16)
    gain_row = lax.broadcasted_iota(jnp.int32, (GAIN_ROWS, H), 0)
    gains = jnp.where(gain_row == 0, row_of(acc), jnp.where(gain_row == 1, gain_n_row, 0.0))
    a_send[4 * H :] = gains.astype(BF16)

    wide = share + GAIN_ROWS
    wide_rows = pl.ds(last * share, wide)
    narrow = pl.ds(0, share)
    is_last = mine == last

    gain_rows = pl.ds(group * share, GAIN_ROWS)
    each_member(lambda i, to: push(a_send.at[shard(i)], a_recv.at[mine, narrow], 2, to))

    @pl.when(jnp.logical_not(is_last))
    def _():
        push(a_send.at[gain_rows], a_recv.at[mine, pl.ds(share, GAIN_ROWS)], 2, member(last))

    @pl.when(is_last)
    def _():
        a_recv[mine] = a_send[wide_rows]

    @pl.when(jnp.logical_not(is_last))
    def _():
        a_recv[mine, 0:share] = a_send[shard(mine)]

    s_T = nt(da, hot[...]).astype(BF16)
    dghost = nn(w1b[H : 2 * H], s_T[:, C:T]).T
    gb_send[0] = (dghost[0:GQ] + dghost[3 * GQ : 4 * GQ]).astype(BF16)
    gb_send[1] = dghost[GQ : 2 * GQ].astype(BF16)
    gb_send[2] = dghost[2 * GQ : 3 * GQ].astype(BF16)
    ghost_back = [
        pltpu.make_async_remote_copy(
            src_ref=gb_send.at[k], dst_ref=gb_recv.at[k], send_sem=bsem_s.at[k], recv_sem=bsem_r.at[k],
            device_id=(to, core), device_id_type=MESH,
        )
        for k, to in enumerate((partner, right, left))
    ]
    for copy in ghost_back:
        copy.start()

    await_bytes(b_others, psem_r.at[0])
    b_lift[level] = jnp.sum(b_recv[...].astype(F32), axis=0).astype(BF16)
    each_level(lambda to: push(b_lift.at[level], b_lift.at[level], 1, to))

    @pl.when(is_last)
    def _():
        await_bytes(a_recv.at[pl.ds(0, group - 1)], psem_r.at[2])
        a_lift[level] = jnp.sum(a_recv[...].astype(F32), axis=0).astype(BF16)
        each_level(lambda to: push(a_lift.at[level], a_lift.at[level], 4, to))

    @pl.when(jnp.logical_not(is_last))
    def _():
        await_bytes(a_recv.at[pl.ds(0, group - 1), narrow], psem_r.at[2])
        a_lift[level, 0:share] = jnp.sum(a_recv[:, 0:share].astype(F32), axis=0).astype(BF16)
        each_level(lambda to: push(a_lift.at[level, narrow], a_lift.at[level, narrow], 4, to))

    dx = nn(w1b[0:H], da).astype(BF16).astype(F32)
    half_e = E // 2
    gedge[0:half_e] = (gT[:, 0:half_e] + dx[:, 0:half_e]).T

    await_bytes(b_levels, psem_r.at[1])
    b_all[mine] = (jnp.sum(b_lift[...].astype(F32), axis=0) * factor).astype(BF16)
    each_member(lambda i, to: push(b_all.at[mine], b_all.at[mine], 3, to))

    gedge[half_e:E] = (gT[:, half_e:E] + dx[:, half_e:E]).T
    own = nn(w1b[H : 2 * H], s_T[:, 0:C]) + nn(w1b[2 * H : 3 * H], s_T[:, T:])
    gnode[...] = (node_T + own).T

    @pl.when(is_last)
    def _():
        await_bytes(a_lift.at[pl.ds(0, depth - 1)], psem_r.at[4])
        total = (jnp.sum(a_lift[...].astype(F32), axis=0) * factor).astype(BF16)
        a_all[wide_rows] = total
        each_member(lambda i, to: push(a_all.at[wide_rows], a_all.at[wide_rows], 5, to))

    @pl.when(jnp.logical_not(is_last))
    def _():
        await_bytes(a_lift.at[pl.ds(0, depth - 1), narrow], psem_r.at[4])
        total = (jnp.sum(a_lift[:, 0:share].astype(F32), axis=0) * factor).astype(BF16)
        a_all[shard(mine)] = total
        each_member(lambda i, to: push(a_all.at[shard(mine)], a_all.at[shard(mine)], 5, to))

    for copy in ghost_back:
        copy.wait_recv()
    back = jnp.concatenate([gb_recv[0], gb_recv[1], gb_recv[2], gb_recv[0]], axis=0)
    gnode[...] += nn(hot_out, back)

    await_bytes(b_shares, psem_r.at[3])
    gn1[...] = b_all[0 : 2 * H // share].astype(F32).reshape(2 * H, H)
    gn2[...] = b_all[2 * H // share : 3 * H // share].astype(F32).reshape(H, H)

    for copy in ghost_out + ghost_back:
        copy.wait_send()
    await_bytes(b_others, psem_s.at[0])
    await_bytes(b_levels, psem_s.at[1])
    await_bytes(b_shares, psem_s.at[3])

    without_share = a_all.at[pl.ds(0, (group - 1) * share)]
    without_gains = a_all.at[pl.ds(0, (group - 1) * share + GAIN_ROWS)]

    @pl.when(is_last)
    def _():
        await_bytes(without_share, psem_s.at[2])
        await_bytes(a_lift.at[pl.ds(0, depth - 1)], psem_s.at[4])
        await_bytes(a_recv.at[pl.ds(0, group - 1)], psem_s.at[5])
        await_bytes(without_share, psem_r.at[5])

    @pl.when(jnp.logical_not(is_last))
    def _():
        await_bytes(without_gains, psem_s.at[2])
        await_bytes(a_lift.at[pl.ds(0, depth - 1), narrow], psem_s.at[4])
        await_bytes(a_recv.at[pl.ds(0, group - 1), narrow], psem_s.at[5])
        await_bytes(without_gains, psem_r.at[5])

    gw1[...] = a_all[0 : 3 * H].astype(F32)
    gw2[...] = a_all[3 * H : 4 * H].astype(F32)
    tail = a_all[4 * H : 4 * H + GAIN_ROWS].astype(F32)
    geg[...] = tail[0:1]
    gng[...] = tail[1:2]


def deliver(*refs):
    n = len(refs) // 2
    sem = refs[-1]
    pairs = []
    for i in range(n):
        src, dst = refs[i], refs[n + i]
        size = src.shape[0]
        if size > 512:
            cuts = [pl.ds(j * size // PIECES, size // PIECES) for j in range(PIECES)]
            pairs += [(src.at[c], dst.at[c]) for c in cuts]
        else:
            pairs.append((src, dst))
    copies = [pltpu.make_async_copy(src, dst, sem.at[i]) for i, (src, dst) in enumerate(pairs)]
    for copy in copies:
        copy.start()
    for copy in copies:
        copy.wait()


def on_device(
    plane, node_feat, edge_feat, cot_node, cot_edge, senders, receivers, send_rows, edge_count,
    edge_w1, edge_w2, edge_gain, node_w1, node_w2, node_gain,
):
    peers, dps = lax.axis_size("morton"), lax.axis_size("dp")
    C, H = node_feat.shape[1:]
    E = edge_feat.shape[1]
    GH = send_rows.shape[1]
    GQ = GH // 4
    T = C + GH
    group = plane * dps
    depth = peers // plane
    share = 4 * H // group
    factor = (dps * peers * E) ** -0.5
    vmem = pl.BlockSpec(memory_space=pltpu.VMEM)
    hbm = pl.BlockSpec(memory_space=pltpu.HBM)
    shape = jax.ShapeDtypeStruct
    dma = pltpu.SemaphoreType.DMA
    results = [
        shape((C, H), F32), shape((E, H), F32), shape((3 * H, H), F32), shape((H, H), F32),
        shape((1, H), F32), shape((2 * H, H), F32), shape((H, H), F32), shape((1, H), F32),
    ]
    args = [
        node_feat[0], send_rows, edge_feat[0], senders, receivers, edge_w1, edge_w2, edge_count,
        edge_gain.reshape(1, H), node_gain.reshape(1, H), node_w1, node_w2, cot_node[0], cot_edge[0],
    ]
    args = [a if a is edge_count else pltpu.with_memory_space_constraint(a, pltpu.HBM) for a in args]
    landing = [pltpu.VMEM(a.shape, a.dtype) for a in args]
    landing[7] = pltpu.SMEM((1, 1), jnp.int32)
    outs = pl.pallas_call(
        functools.partial(kernel, (peers, dps, plane, factor)),
        out_shape=results,
        in_specs=[hbm] * 14,
        out_specs=[vmem] * 8,
        scratch_shapes=landing + [
            dma((14,)),
            pltpu.VMEM((T + C, E), BF16), pltpu.VMEM((3 * H, E), BF16), pltpu.VMEM((H, E), BF16),
            pltpu.VMEM((H, E), F32), pltpu.VMEM((H, E), F32),
            pltpu.VMEM((H, E), F32), pltpu.VMEM((H, E), F32), pltpu.VMEM((H, E), F32),
            pltpu.VMEM((3, GQ, H), BF16), pltpu.VMEM((3, GQ, H), BF16),
            pltpu.VMEM((3, GQ, H), BF16), pltpu.VMEM((3, GQ, H), BF16),
            dma((3,)), dma((3,)), dma((3,)), dma((3,)),
            pltpu.VMEM((4 * H + GAIN_ROWS, H), BF16), pltpu.VMEM((group, share + GAIN_ROWS, H), BF16),
            pltpu.VMEM((depth, share + GAIN_ROWS, H), BF16), pltpu.VMEM((4 * H + GAIN_ROWS, H), BF16),
            pltpu.VMEM((4 * H, H), BF16), pltpu.VMEM((group, share, H), BF16),
            pltpu.VMEM((depth, share, H), BF16), pltpu.VMEM((group, share, H), BF16),
            dma((6,)), dma((6,)),
        ],
        compiler_params=pltpu.CompilerParams(
            collective_id=0, has_side_effects=True, vmem_limit_bytes=40 * 1024 * 1024
        ),
    )(*args)
    outs = [pltpu.with_memory_space_constraint(a, pltpu.VMEM) for a in outs]
    outs = pl.pallas_call(
        deliver,
        out_shape=results,
        in_specs=[vmem] * 8,
        out_specs=[hbm] * 8,
        scratch_shapes=[dma((7 + PIECES,))],
    )(*outs)
    return (
        outs[0][None], outs[1][None], outs[2], outs[3], outs[4].reshape(H), outs[5], outs[6], outs[7].reshape(H)
    )


def solution(mesh):
    cells = P("dp", "morton", None)
    flat = P("dp", "morton")
    plane = min(16, mesh.shape["morton"] // 2)
    return jax.shard_map(
        functools.partial(on_device, plane),
        mesh=mesh,
        in_specs=(cells, cells, cells, cells, flat, flat, flat, flat, P(), P(), P(), P(), P(), P()),
        out_specs=(cells, cells, P(), P(), P(), P(), P(), P()),
        check_vma=False,
    )
```
